32 devices in a mesh: groups: 2 (over y), latent: 8 (over z, x), hidden: 2 (over core).
Axes of the slice: x: 2, y: 2, z: 4, core: 2. Of those that a mesh axis runs over, the one named last changes fastest.
Arguments:
- tokens: bfloat16 [32, 8192], P(('groups', 'latent'), 'hidden'), parts along dimension 0, may hold values from -6 to 6
- b_dec: float32 [16384], P(('groups', 'hidden')), parts along dimension 0, may hold values from -3 to 3
- w_enc: bfloat16 [2048, 8192], P(('groups', 'latent'), 'hidden'), parts along dimension 0
- b_enc: float32 [2048], P(('groups', 'latent')), parts along dimension 0, may hold values from -3 to 3
- w_dec: bfloat16 [2048, 8192], P(('groups', 'latent'), 'hidden'), parts along dimension 0
- bias_moments: float32 [2, 2048], P(None, ('groups', 'latent')), parts along dimension 1, may hold values from 0.001 to 1
- pool: bfloat16 [128, 8192], P(('groups', 'latent'), 'hidden'), parts along dimension 0, may hold values from -6 to 6
- active_blocks: int32 [8, 16], P('groups'), parts along dimension 0, may hold values from 0 to 31, as said below
- dead_ids: int32 [64], P('groups'), parts along dimension 0, may hold values from 0 to 1023, as said below
- row_ids: int32 [64], P('groups'), parts along dimension 0, may hold values from 0 to 63, as said below
Outputs:
- losses: float32 [32], P(('groups', 'latent')), parts along dimension 0
- new_enc: bfloat16 [2048, 8192], P(('groups', 'latent'), 'hidden'), parts along dimension 0
- new_dec: bfloat16 [2048, 8192], P(('groups', 'latent'), 'hidden'), parts along dimension 0
- new_b_enc: float32 [2048], P(('groups', 'latent')), parts along dimension 0
- new_moments: float32 [2, 2048], P(None, ('groups', 'latent')), parts along dimension 1
The draws below stay inside these ranges and needn't reach their ends.
There are 2 independent parts, one for each index of `groups`. The reference program is written for one: setup_inputs(seed, part) draws one part's arguments, and reference() takes and returns one part's arrays. A program takes and returns all parts, laid end to end along the dimension named above; each array names one. Nothing has to cross between parts.
Inputs may be any that keep to these rules, and one draw needn't show every extreme that they name: `active_blocks`: each row names 16 distinct blocks. `dead_ids`: distinct latents; latent index i owns latents i * 128 to (i + 1) * 128 - 1, at most 8 of them are dead, and some index has exactly that many. `row_ids`: row r is held by latent index r // 8; the dead latents of one latent index take their rows from distinct holding indices; a row may serve several dead latents.
All inputs are finite; a program needn't handle non-finite values.
Results may differ from the reference program's by a relative error of at most 0.0004.
The reference program's roundings to bfloat16 on the way (of `centered` and `latent_codes`) count: a program that leaves them out, or rounds other values in their place, can miss the bound.
Values may be sent and summed in bfloat16 or wider, within the bound.
No kernel may reach another device: no remote copies, remote signals or barrier semaphores. Data moves between devices by JAX's collectives and lax.ppermute only.
A program may use at most 64 MiB of HBM per device.

```python
import math
import jax
import jax.numpy as jnp
from jax import lax

D = 8192
LAT_DEV = 128
BLOCK = 32
TILES = 4
DEAD_DEV = 4
POOL_DEV = 8
LATENTS = 1024
NBLK = 32
ACT = 16
TOKENS = 16
DEAD = 32
POOL = 64


def dead_plan(key):
    owners = LATENTS // LAT_DEV
    most = 2 * DEAD_DEV
    keys = jax.random.split(key, 6)
    owner_order = jax.random.permutation(keys[0], owners)
    halfway = owners // 2
    spread = jax.random.randint(keys[1], (halfway,), 0, DEAD_DEV + 1).at[0].set(DEAD_DEV)
    counts = jnp.zeros((owners,), jnp.int32)
    counts = counts.at[owner_order[:halfway]].set(DEAD_DEV + spread)
    counts = counts.at[owner_order[halfway:]].set(DEAD_DEV - spread)
    local_scores = jax.random.randint(keys[2], (owners, LAT_DEV), 0, 1 << 20) * LAT_DEV + jnp.arange(LAT_DEV)[None, :]
    local_pick = lax.top_k(local_scores, most)[1]
    holder_scores = jax.random.randint(keys[3], (owners, owners), 0, 1 << 20) * owners + jnp.arange(owners)[None, :]
    holders = lax.top_k(holder_scores, most)[1]
    slots = jax.random.randint(keys[4], (owners, most), 0, POOL_DEV)
    latent_ids = jnp.arange(owners)[:, None] * LAT_DEV + local_pick
    chosen_rows = holders * POOL_DEV + slots
    unused = (jnp.arange(most)[None, :] >= counts[:, None]).astype(jnp.int32).reshape(-1)
    keep_order = jnp.argsort(unused, stable=True)[:DEAD]
    shuffle = jax.random.permutation(keys[5], DEAD)
    picked = keep_order[shuffle]
    return (latent_ids.reshape(-1)[picked].astype(jnp.int32), chosen_rows.reshape(-1)[picked].astype(jnp.int32))


def draw_dead_ids(key, part):
    return dead_plan(key)[0]


def draw_row_ids(key, part):
    return dead_plan(key)[1]


def draw_active_blocks(key, part):
    key = jax.random.fold_in(key, 11)
    first_key, second_key = jax.random.split(key)
    owners = LATENTS // LAT_DEV
    popular = jax.random.randint(first_key, (owners,), 0, 4)
    popular = popular.at[0].set(3).at[owners - 1].set(3)
    block_pop = jnp.repeat(popular, LAT_DEV // BLOCK)
    noise = jax.random.randint(second_key, (TILES, NBLK), 0, 8192)
    scores = (block_pop[None, :] * 4096 + noise) * NBLK + jnp.arange(NBLK)[None, :]
    return lax.top_k(scores, ACT)[1].astype(jnp.int32)


def draw_w_enc(key, part):
    key = jax.random.fold_in(key, 3)
    first_key, second_key = jax.random.split(key, 2)
    position = jnp.arange(LATENTS, dtype=jnp.float32) / LATENTS
    base = jax.random.normal(first_key, (LATENTS, D), jnp.float32)
    scales = jnp.exp(jax.random.uniform(second_key, (LATENTS,), jnp.float32, math.log(0.3), math.log(3.0)))
    factor = scales * (1.0 + 2.0 * position) / math.sqrt(D)
    return (base * factor[:, None]).astype(jnp.bfloat16)


def draw_w_dec(key, part):
    key = jax.random.fold_in(key, 5)
    first_key, second_key = jax.random.split(key, 2)
    base = jax.random.normal(first_key, (LATENTS, D), jnp.float32)
    scales = jnp.exp(jax.random.uniform(second_key, (LATENTS,), jnp.float32, math.log(0.3), math.log(3.0)))
    return (base * (scales / math.sqrt(D))[:, None]).astype(jnp.bfloat16)


def shard_levels(own_key, shape, cuts, least, high):
    factor_of, own = 1.0, jax.random.fold_in(own_key, 6)
    for axis_at, shards_of in cuts:
        draws = jnp.exp(jax.random.uniform(jax.random.fold_in(own, axis_at), (shards_of,), jnp.float32, least / len(cuts), high / len(cuts)))
        factor_of = factor_of * jnp.repeat(draws, shape[axis_at] // shards_of).reshape([-1 if axis == axis_at else 1 for axis in range(len(shape))])
    return factor_of


def gaussian(rng, shape, deviation, most, pieces=(), kind=jnp.bfloat16):
    loudness = shard_levels(rng, shape, pieces, -0.22, 0.18) if pieces else 1.0
    entries = jax.random.normal(rng, shape, jnp.float32) * deviation * loudness
    return jnp.minimum(jnp.maximum(entries, -most), most).astype(kind)


def setup_inputs(seed: int = 0, part: int = 0) -> dict:
    splits = jax.random.split(jax.random.key(seed), 11)
    own_keys = jax.random.split(jax.random.fold_in(splits[10], part), 11)
    tokens = gaussian(own_keys[0], (TOKENS, D), 1.0, 6.0, ((0, 8), (1, 2)))
    b_dec = gaussian(own_keys[1], (D,), 0.5, 3.0, ((0, 2),), jnp.float32)
    w_enc = draw_w_enc(jax.random.fold_in(jax.random.fold_in(splits[10], part), 71), part)
    b_enc = gaussian(own_keys[3], (LATENTS,), 0.5, 3.0, ((0, 8),), jnp.float32)
    w_dec = draw_w_dec(jax.random.fold_in(jax.random.fold_in(splits[10], part), 71), part)
    bias_moments = jnp.clip(jnp.exp(math.log(1.0) - 6.9077552 * jax.random.uniform(own_keys[5], (2, LATENTS), jnp.float32) ** shard_levels(own_keys[5], (2, LATENTS), ((1, 8),), -0.2, 0.2)), 0.001, 1.0)
    pool = gaussian(own_keys[6], (POOL, D), 1.0, 6.0, ((0, 8), (1, 2)))
    active_blocks = draw_active_blocks(jax.random.fold_in(jax.random.fold_in(splits[10], part), 71), part)
    dead_ids = draw_dead_ids(jax.random.fold_in(jax.random.fold_in(splits[10], part), 71), part)
    row_ids = draw_row_ids(jax.random.fold_in(jax.random.fold_in(splits[10], part), 71), part)
    return dict(tokens=tokens, b_dec=b_dec, w_enc=w_enc, b_enc=b_enc, w_dec=w_dec, bias_moments=bias_moments, pool=pool, active_blocks=active_blocks, dead_ids=dead_ids, row_ids=row_ids)


epsilon = 1e-06

def reference(tokens, b_dec, w_enc, b_enc, w_dec, bias_moments, pool, active_blocks, dead_ids, row_ids):
    tokens_wide = tokens.astype(jnp.float32)
    centered = (tokens_wide - b_dec[None, :]).astype(jnp.bfloat16)
    pre_act = lax.dot_general(centered, w_enc, (((1,), (1,)), ((), ())), preferred_element_type=jnp.float32) + b_enc[None, :]
    tile_of = jnp.arange(TOKENS) // (TOKENS // TILES)
    block_of = jnp.arange(LATENTS) // BLOCK
    tile_mask = jnp.zeros((TILES, NBLK), jnp.float32).at[jnp.arange(TILES)[:, None], active_blocks].set(1.0)
    full_mask = tile_mask[tile_of][:, block_of]
    latent_codes = (jnp.maximum(pre_act, 0.0) * full_mask).astype(jnp.bfloat16)
    rebuilt = jnp.dot(latent_codes, w_dec, preferred_element_type=jnp.float32) + b_dec[None, :]
    dec_sq = lax.optimization_barrier(jnp.sum(jnp.square(w_dec.astype(jnp.float32)), axis=1))
    enc_sq = lax.optimization_barrier(jnp.sum(jnp.square(w_enc.astype(jnp.float32)), axis=1))
    dec_norm = jnp.sqrt(dec_sq)
    enc_norm = jnp.sqrt(enc_sq)
    penalty = jnp.dot(latent_codes.astype(jnp.float32), dec_norm, precision=lax.Precision.HIGHEST)
    error_mean = lax.optimization_barrier(jnp.mean(jnp.square(tokens_wide - rebuilt), axis=1))
    input_mean = lax.optimization_barrier(jnp.mean(jnp.square(tokens_wide - b_dec[None, :]), axis=1))
    losses = error_mean / (input_mean + epsilon) + 5.0 * penalty / LATENTS
    is_dead = jnp.zeros((LATENTS,), jnp.float32).at[dead_ids].set(1.0)
    alive_mean = jnp.sum(enc_norm * (1.0 - is_dead)) / (LATENTS - DEAD)
    fresh_rows = pool[row_ids].astype(jnp.float32) - b_dec[None, :]
    unit_rows = fresh_rows * lax.rsqrt(lax.optimization_barrier(jnp.sum(fresh_rows * fresh_rows, axis=1)) + epsilon)[:, None]
    new_enc = w_enc.at[dead_ids].set((0.2 * alive_mean * unit_rows).astype(jnp.bfloat16))
    alive_dec = (w_dec.astype(jnp.float32) * lax.rsqrt(dec_sq + epsilon)[:, None]).astype(jnp.bfloat16)
    dead_dec = unit_rows * lax.rsqrt(lax.optimization_barrier(jnp.sum(unit_rows * unit_rows, axis=1)) + epsilon)[:, None]
    new_dec = alive_dec.at[dead_ids].set(dead_dec.astype(jnp.bfloat16))
    new_b_enc = b_enc * (1.0 - is_dead)
    new_moments = bias_moments * (1.0 - is_dead)[None, :]
    return (losses, new_enc, new_dec, new_b_enc, new_moments)
```

```python
import jax
import jax.numpy as jnp
from jax import lax
from jax.sharding import PartitionSpec as P

BLOCK = 32
EPS = 1e-06
F32, BF16 = jnp.float32, jnp.bfloat16


def swap(x, axis, mask):
    size = lax.axis_size(axis)
    return lax.ppermute(x, axis, [(i, i ^ mask) for i in range(size)])


def halves(x):
    high = lax.reduce_precision(x, 8, 7)
    return high.astype(BF16), (x - high).astype(BF16)


def local(tokens, b_dec, w_enc, b_enc, w_dec, bias_moments, pool, active_blocks, dead_ids, row_ids):
    lat_dev, width = w_enc.shape
    owners = lax.axis_size("latent")
    me = lax.axis_index("latent")
    tok_dev, pool_dev = tokens.shape[0], pool.shape[0]
    latents, count = lat_dev * owners, tok_dev * owners
    dead = dead_ids.shape[0]
    tiles = active_blocks.shape[0]
    masks = []
    while 1 << len(masks) < owners:
        masks.append(1 << len(masks))
    order = [0]
    for mask in reversed(masks):
        order = order + [i ^ mask for i in order]
    peer = me ^ jnp.array(order, jnp.int32)

    owner_of, holder_of = dead_ids // lat_dev, row_ids // pool_dev
    slots = me * pool_dev + jnp.arange(pool_dev, dtype=jnp.int32)
    take = jnp.any(
        (owner_of[None, None, :] == peer[:, None, None]) & (row_ids[None, None, :] == slots[None, :, None]),
        axis=2,
    ).astype(BF16)
    rows = jnp.dot(take, pool, preferred_element_type=F32).astype(BF16)

    gathered = tokens
    rows = rows.reshape((2,) * len(masks) + (width,))
    for step, mask in enumerate(reversed(masks)):
        axis = len(masks) - 1 - step
        kept, sent = lax.index_in_dim(rows, 0, axis), lax.index_in_dim(rows, 1, axis)
        n_tok = gathered.shape[0]
        got = swap(jnp.concatenate([gathered, sent.reshape(-1, width)], axis=0), "latent", mask)
        gathered = jnp.concatenate([gathered, got[:n_tok]], axis=0)
        rows = jnp.concatenate([kept, got[n_tok:].reshape(kept.shape)], axis=axis)
    rows = rows.reshape(owners, width)

    local_ids = me * lat_dev + jnp.arange(lat_dev, dtype=jnp.int32)
    dead_hit = dead_ids[None, :] == local_ids[:, None]
    is_dead = jnp.any(dead_hit, axis=1)
    place = jnp.any(dead_hit[:, None, :] & (holder_of[None, None, :] == peer[None, :, None]), axis=2).astype(BF16)

    centered = (gathered.astype(F32) - b_dec[None, :]).astype(BF16)
    partial_pre = lax.dot_general(centered, w_enc, (((1,), (1,)), ((), ())), preferred_element_type=F32)
    dec_wide = w_dec.astype(F32)
    dec_part = jnp.sum(dec_wide * dec_wide, axis=1)
    enc_part = jnp.sum(jnp.square(w_enc.astype(F32)), axis=1)
    fresh = rows.astype(F32) - b_dec[None, :]
    fresh_part = jnp.sum(fresh * fresh, axis=1)
    own_centered = tokens.astype(F32) - b_dec[None, :]
    input_part = jnp.sum(own_centered * own_centered, axis=1)
    tail = jnp.concatenate([fresh_part, input_part])
    pad = -tail.shape[0] % lat_dev
    tail = jnp.pad(tail, (0, pad)).reshape(-1, lat_dev)
    message = jnp.concatenate([partial_pre, dec_part[None], enc_part[None], tail], axis=0)
    total = message + swap(message, "hidden", 1)
    pre = total[:count] + b_enc[None, :]
    dec_sq, enc_sq = total[count], total[count + 1]
    tail = total[count + 2 :].reshape(-1)
    fresh_sq, input_sum = tail[:owners], tail[owners : owners + tok_dev]

    row_tile = (peer[:, None] * tok_dev + jnp.arange(tok_dev, dtype=jnp.int32)[None, :]).reshape(-1) // (count // tiles)
    my_block = local_ids // BLOCK
    listed = jnp.any(active_blocks[:, :, None] == my_block[None, None, :], axis=1).astype(F32)
    mask = jnp.zeros((count, lat_dev), F32)
    for tile in range(tiles):
        mask = jnp.where(row_tile[:, None] == tile, listed[tile][None, :], mask)
    codes = lax.reduce_precision(jnp.maximum(pre, 0.0) * mask, 8, 7)
    dec_norm = jnp.sqrt(dec_sq)
    enc_norm = jnp.sqrt(enc_sq)
    side = jnp.concatenate(
        [codes * dec_norm[None, :], jnp.broadcast_to(jnp.where(is_dead, 0.0, enc_norm)[None, :], (count, lat_dev))], axis=1
    )
    rebuilt = jnp.dot(codes.astype(BF16), w_dec, preferred_element_type=F32)
    for mask_bit in masks:
        half = rebuilt.shape[0] // 2
        high, low = halves(side[half:])
        got = swap(jnp.concatenate([rebuilt[half:].astype(BF16), high, low], axis=1), "latent", mask_bit).astype(F32)
        rebuilt = rebuilt[:half] + got[:, :width]
        side = side[:half] + (got[:, width : width + 2 * lat_dev] + got[:, width + 2 * lat_dev :])
    penalty = jnp.sum(side[:, :lat_dev], axis=1)
    alive = jnp.sum(side[:1, lat_dev:], axis=1, keepdims=True)

    residual = own_centered - rebuilt
    error_part = jnp.sum(residual * residual, axis=1)
    error_sum = error_part + swap(error_part, "hidden", 1)
    full = width * lax.axis_size("hidden")
    losses = error_sum / full / (input_sum / full + EPS) + 5.0 * penalty / latents

    alive_mean = alive / (latents - dead)
    unit = fresh * lax.rsqrt(fresh_sq + EPS)[:, None]
    enc_rows = (0.2 * alive_mean * unit).astype(BF16)
    unit_sq = fresh_sq / (fresh_sq + EPS)
    dec_rows = (unit * lax.rsqrt(unit_sq + EPS)[:, None]).astype(BF16)
    placed_dec = jnp.dot(place, dec_rows, preferred_element_type=F32)
    new_dec = jnp.where(is_dead[:, None], placed_dec, dec_wide * lax.rsqrt(dec_sq + EPS)[:, None]).astype(BF16)
    placed_enc = jnp.dot(place, enc_rows, preferred_element_type=F32).astype(BF16)
    new_enc = jnp.where(is_dead[:, None], placed_enc, w_enc)
    keep = jnp.where(is_dead, 0.0, 1.0)
    return losses, new_enc, new_dec, b_enc * keep, bias_moments * keep[None, :]


def solution(mesh):
    both = P(("groups", "latent"), "hidden")
    one = P(("groups", "latent"))
    return jax.shard_map(
        local,
        mesh=mesh,
        in_specs=(both, P(("groups", "hidden")), both, one, both, P(None, ("groups", "latent")), both,
                  P("groups", None), P("groups"), P("groups")),
        out_specs=(one, both, both, one, P(None, ("groups", "latent"))),
        check_vma=False,
    )
```

```python
import jax
import jax.numpy as jnp
from jax import lax
from jax.experimental import pallas as pl
from jax.experimental.pallas import tpu as pltpu
from jax.sharding import PartitionSpec as P

BLOCK = 32
EPS = 1e-06
F32, BF16 = jnp.float32, jnp.bfloat16


def swap(x):
    return lax.ppermute(x, "hidden", [(0, 1), (1, 0)])


def outgoing(tokens, pool, dead_ids, row_ids, owners, lat_dev):
    tok_dev, width = tokens.shape
    pool_dev, dead = pool.shape[0], dead_ids.shape[1]
    part = width // tok_dev

    def body(tokens_ref, pool_ref, dead_ref, row_ref, out_ref):
        me = lax.axis_index("latent")
        first = lax.broadcasted_iota(jnp.int32, (owners, dead), 0) * lat_dev
        there = (dead_ref[...] >= first) & (dead_ref[...] < first + lat_dev)
        slot = lax.broadcasted_iota(jnp.int32, (pool_dev, dead), 0) + me * pool_dev
        goes = jnp.where(there, 1.0, 0.0).astype(BF16)
        lies = jnp.where(row_ref[...] == slot, 1.0, 0.0).astype(BF16)
        take = lax.dot_general(goes, lies, (((1,), (1,)), ((), ())), preferred_element_type=F32).astype(BF16)
        rows = jnp.dot(take, pool_ref[...], preferred_element_type=F32)
        for dest in range(owners):
            out_ref[dest, :, :width] = tokens_ref[...]
        for piece in range(tok_dev):
            out_ref[:, piece, width:] = rows[:, piece * part : (piece + 1) * part].astype(BF16)

    return pl.pallas_call(
        body,
        out_shape=jax.ShapeDtypeStruct((owners, tok_dev, width + part), BF16),
        in_specs=[pl.BlockSpec(memory_space=pltpu.VMEM)] * 4,
        out_specs=pl.BlockSpec(memory_space=pltpu.VMEM),
        name="outgoing",
    )(tokens, pool, dead_ids, row_ids)


def local(tokens, b_dec, w_enc, b_enc, w_dec, bias_moments, pool, active_blocks, dead_ids, row_ids):
    lat_dev, width = w_enc.shape
    owners = lax.axis_size("latent")
    me = lax.axis_index("latent")
    tok_dev, pool_dev = tokens.shape[0], pool.shape[0]
    latents, count = lat_dev * owners, tok_dev * owners
    dead = dead_ids.shape[0]
    tiles = active_blocks.shape[0]
    part = width // tok_dev
    holder_of = row_ids // pool_dev
    everyone = jnp.arange(owners, dtype=jnp.int32)
    sent = outgoing(tokens, pool, dead_ids[None], row_ids[None], owners, lat_dev)
    got = lax.all_to_all(sent, "latent", 0, 0)

    local_ids = me * lat_dev + jnp.arange(lat_dev, dtype=jnp.int32)
    dead_hit = dead_ids[None, :] == local_ids[:, None]
    is_dead = jnp.any(dead_hit, axis=1)
    place = lax.dot_general(
        dead_hit.astype(BF16), (holder_of[None, :] == everyone[:, None]).astype(BF16),
        (((1,), (1,)), ((), ())), preferred_element_type=F32).astype(BF16)
    keep = jnp.where(is_dead, 0.0, 1.0)
    new_b_enc = b_enc * keep
    new_moments = bias_moments * keep[None, :]
    row_tile = jnp.arange(count, dtype=jnp.int32) // (count // tiles)
    my_block = local_ids // BLOCK
    listed = jnp.any(active_blocks[:, :, None] == my_block[None, None, :], axis=1).astype(F32)
    mask = jnp.zeros((count, lat_dev), F32)
    for tile in range(tiles):
        mask = jnp.where(row_tile[:, None] == tile, listed[tile][None, :], mask)
    dec_wide = w_dec.astype(F32)
    dec_part = jnp.sum(dec_wide * dec_wide, axis=1)
    enc_part = jnp.sum(jnp.square(w_enc.astype(F32)), axis=1)
    own_centered = tokens.astype(F32) - b_dec[None, :]
    input_part = jnp.sum(own_centered * own_centered, axis=1)
    centered = (got[:, :, :width].astype(F32) - b_dec[None, None, :]).astype(BF16).reshape(count, width)
    partial_pre = lax.dot_general(centered, w_enc, (((1,), (1,)), ((), ())), preferred_element_type=F32)
    fresh = got[:, :, width:].astype(F32) - b_dec.reshape(tok_dev, part)[None]
    tail = jnp.concatenate([jnp.sum(fresh * fresh, axis=(1, 2)), input_part])
    tail = jnp.pad(tail, (0, -tail.shape[0] % lat_dev)).reshape(-1, lat_dev)
    message = jnp.concatenate([partial_pre, dec_part[None], enc_part[None], tail], axis=0)
    total = message + swap(message)
    pre = total[:count] + b_enc[None, :]
    dec_sq, enc_sq = total[count], total[count + 1]
    tail = total[count + 2 :].reshape(-1)
    fresh_sq, input_sum = tail[:owners], tail[owners : owners + tok_dev]

    codes = lax.reduce_precision(jnp.maximum(pre, 0.0) * mask, 8, 7)
    norms = jnp.where(is_dead, 0.0, jnp.sqrt(enc_sq))
    side = jnp.concatenate(
        [codes * jnp.sqrt(dec_sq)[None, :], jnp.broadcast_to(norms[None, :], (count, lat_dev))], axis=1)
    high = lax.reduce_precision(side, 8, 7)
    rebuilt = jnp.dot(codes.astype(BF16), w_dec, preferred_element_type=F32)
    sent = jnp.concatenate([rebuilt.astype(BF16), high.astype(BF16), (side - high).astype(BF16)], axis=1)
    summed = lax.all_to_all(sent.reshape(owners, tok_dev, -1), "latent", 0, 0)

    unit = fresh * lax.rsqrt(fresh_sq + EPS)[:, None, None]
    unit_sq = fresh_sq / (fresh_sq + EPS)
    dec_rows = (unit * lax.rsqrt(unit_sq + EPS)[:, None, None]).astype(BF16).reshape(owners, width)
    placed_dec = jnp.dot(place, dec_rows, preferred_element_type=F32)
    new_dec = jnp.where(is_dead[:, None], placed_dec, dec_wide * lax.rsqrt(dec_sq + EPS)[:, None]).astype(BF16)
    summed, new_dec, unit = lax.optimization_barrier((summed, new_dec, unit))

    summed = jnp.sum(summed.astype(F32), axis=0)
    residual = own_centered - summed[:, :width]
    error_part = jnp.sum(jnp.square(residual).reshape(tok_dev, -1, 128), axis=1)
    error_peer = swap(error_part)
    side = summed[:, width : width + 2 * lat_dev] + summed[:, width + 2 * lat_dev :]
    alive_mean = jnp.sum(side[:, lat_dev:], axis=1) / (latents - dead)
    enc_rows = ((0.2 * alive_mean)[None, :, None] * unit).astype(BF16).reshape(owners, width)
    placed_enc = jnp.dot(place, enc_rows, preferred_element_type=F32).astype(BF16)
    new_enc = jnp.where(is_dead[:, None], placed_enc, w_enc)
    penalty = jnp.sum(side[:, :lat_dev], axis=1)
    error_sum = jnp.sum(error_part + error_peer, axis=1)
    full = width * lax.axis_size("hidden")
    losses = error_sum / full / (input_sum / full + EPS) + 5.0 * penalty / latents
    return losses, new_enc, new_dec, new_b_enc, new_moments


def solution(mesh):
    both = P(("groups", "latent"), "hidden")
    one = P(("groups", "latent"))
    return jax.shard_map(
        local,
        mesh=mesh,
        in_specs=(both, P(("groups", "hidden")), both, one, both, P(None, ("groups", "latent")), both,
                  P("groups", None), P("groups"), P("groups")),
        out_specs=(one, both, both, one, P(None, ("groups", "latent"))),
        check_vma=False,
    )
```

```python
import jax
import jax.numpy as jnp
from jax import lax
from jax.experimental import pallas as pl
from jax.experimental.pallas import tpu as pltpu
from jax.sharding import PartitionSpec as P

BLOCK = 32
EPS = 1e-06
F32, BF16 = jnp.float32, jnp.bfloat16


def swap(x):
    return lax.ppermute(x, "hidden", [(0, 1), (1, 0)])


def middle_out(owners):
    return sorted(range(owners), key=lambda i: (abs(4 * (i // 2) - owners + 2), i // 2, abs(2 * i - owners + 1)))


def outgoing(tokens, pool, dead_ids, row_ids, firsts, lat_dev):
    tok_dev, width = tokens.shape
    pool_dev, owners = pool.shape[0], firsts.shape[0]
    dead = dead_ids.shape[1]
    part = width // tok_dev

    def body(tokens_ref, pool_ref, dead_ref, row_ref, firsts_ref, out_ref):
        me = lax.axis_index("latent")
        first = firsts_ref[...]
        there = (dead_ref[...] >= first) & (dead_ref[...] < first + lat_dev)
        slot = lax.broadcasted_iota(jnp.int32, (pool_dev, dead), 0) + me * pool_dev
        goes = jnp.where(there, 1.0, 0.0).astype(BF16)
        lies = jnp.where(row_ref[...] == slot, 1.0, 0.0).astype(BF16)
        take = lax.dot_general(goes, lies, (((1,), (1,)), ((), ())), preferred_element_type=F32).astype(BF16)
        rows = jnp.dot(take, pool_ref[...], preferred_element_type=F32)
        for dest in range(owners):
            out_ref[dest, :, :width] = tokens_ref[...]
        for piece in range(tok_dev):
            out_ref[:, piece, width:] = rows[:, piece * part : (piece + 1) * part].astype(BF16)

    return pl.pallas_call(
        body,
        out_shape=jax.ShapeDtypeStruct((owners, tok_dev, width + part), BF16),
        in_specs=[pl.BlockSpec(memory_space=pltpu.VMEM)] * 5,
        out_specs=pl.BlockSpec(memory_space=pltpu.VMEM),
        name="outgoing",
    )(tokens, pool, dead_ids, row_ids, firsts)


def local(tokens, b_dec, w_enc, b_enc, w_dec, bias_moments, pool, active_blocks, dead_ids, row_ids):
    lat_dev, width = w_enc.shape
    owners = lax.axis_size("latent")
    me = lax.axis_index("latent")
    tok_dev, pool_dev = tokens.shape[0], pool.shape[0]
    latents, count = lat_dev * owners, tok_dev * owners
    dead = dead_ids.shape[0]
    tiles = active_blocks.shape[0]
    part = width // tok_dev
    holder_of = row_ids // pool_dev
    order = middle_out(owners)
    everyone = jnp.array(order, jnp.int32)
    sent = outgoing(tokens, pool, dead_ids[None], row_ids[None], everyone[:, None] * lat_dev, lat_dev)
    got = lax.all_to_all(sent, "latent", 0, 0, axis_index_groups=[order])

    local_ids = me * lat_dev + jnp.arange(lat_dev, dtype=jnp.int32)
    dead_hit = dead_ids[None, :] == local_ids[:, None]
    is_dead = jnp.any(dead_hit, axis=1)
    place = lax.dot_general(
        dead_hit.astype(BF16), (holder_of[None, :] == everyone[:, None]).astype(BF16),
        (((1,), (1,)), ((), ())), preferred_element_type=F32).astype(BF16)
    keep = jnp.where(is_dead, 0.0, 1.0)
    new_b_enc = b_enc * keep
    new_moments = bias_moments * keep[None, :]
    row_tile = jnp.repeat(everyone, tok_dev) // (owners // tiles)
    my_block = local_ids // BLOCK
    listed = jnp.any(active_blocks[:, :, None] == my_block[None, None, :], axis=1).astype(F32)
    mask = jnp.zeros((count, lat_dev), F32)
    for tile in range(tiles):
        mask = jnp.where(row_tile[:, None] == tile, listed[tile][None, :], mask)
    dec_wide = w_dec.astype(F32)
    dec_part = jnp.sum(dec_wide * dec_wide, axis=1)
    enc_part = jnp.sum(jnp.square(w_enc.astype(F32)), axis=1)
    own_centered = tokens.astype(F32) - b_dec[None, :]
    input_part = jnp.sum(own_centered * own_centered, axis=1)
    centered = (got[:, :, :width].astype(F32) - b_dec[None, None, :]).astype(BF16).reshape(count, width)
    partial_pre = lax.dot_general(centered, w_enc, (((1,), (1,)), ((), ())), preferred_element_type=F32)
    fresh = got[:, :, width:].astype(F32) - b_dec.reshape(tok_dev, part)[None]
    tail = jnp.concatenate([jnp.sum(fresh * fresh, axis=(1, 2)), input_part])
    tail = jnp.pad(tail, (0, -tail.shape[0] % lat_dev)).reshape(-1, lat_dev)
    message = jnp.concatenate([partial_pre, dec_part[None], enc_part[None], tail], axis=0)
    total = message + swap(message)
    pre = total[:count] + b_enc[None, :]
    dec_sq, enc_sq = total[count], total[count + 1]
    tail = total[count + 2 :].reshape(-1)
    fresh_sq, input_sum = tail[:owners], tail[owners : owners + tok_dev]

    codes = lax.reduce_precision(jnp.maximum(pre, 0.0) * mask, 8, 7)
    norms = jnp.where(is_dead, 0.0, jnp.sqrt(enc_sq))
    side = jnp.concatenate(
        [codes * jnp.sqrt(dec_sq)[None, :], jnp.broadcast_to(norms[None, :], (count, lat_dev))], axis=1)
    high = lax.reduce_precision(side, 8, 7)
    rebuilt = jnp.dot(codes.astype(BF16), w_dec, preferred_element_type=F32)
    sent = jnp.concatenate([rebuilt.astype(BF16), high.astype(BF16), (side - high).astype(BF16)], axis=1)
    summed = lax.all_to_all(sent.reshape(owners, tok_dev, -1), "latent", 0, 0, axis_index_groups=[order])

    unit = fresh * lax.rsqrt(fresh_sq + EPS)[:, None, None]
    unit_sq = fresh_sq / (fresh_sq + EPS)
    dec_rows = (unit * lax.rsqrt(unit_sq + EPS)[:, None, None]).astype(BF16).reshape(owners, width)
    placed_dec = jnp.dot(place, dec_rows, preferred_element_type=F32)
    new_dec = jnp.where(is_dead[:, None], placed_dec, dec_wide * lax.rsqrt(dec_sq + EPS)[:, None]).astype(BF16)
    summed, new_dec, unit = lax.optimization_barrier((summed, new_dec, unit))

    summed = jnp.sum(summed.astype(F32), axis=0)
    residual = own_centered - summed[:, :width]
    error_part = jnp.sum(jnp.square(residual).reshape(tok_dev, -1, 128), axis=1)
    error_peer = swap(error_part)
    side = summed[:, width : width + 2 * lat_dev] + summed[:, width + 2 * lat_dev :]
    alive_mean = jnp.sum(side[:, lat_dev:], axis=1) / (latents - dead)
    enc_rows = ((0.2 * alive_mean)[None, :, None] * unit).astype(BF16).reshape(owners, width)
    placed_enc = jnp.dot(place, enc_rows, preferred_element_type=F32).astype(BF16)
    new_enc = jnp.where(is_dead[:, None], placed_enc, w_enc)
    error_peer, new_enc = lax.optimization_barrier((error_peer, new_enc))
    penalty = jnp.sum(side[:, :lat_dev], axis=1)
    error_sum = jnp.sum(error_part + error_peer, axis=1)
    full = width * lax.axis_size("hidden")
    losses = error_sum / full / (input_sum / full + EPS) + 5.0 * penalty / latents
    return losses, new_enc, new_dec, new_b_enc, new_moments


def solution(mesh):
    both = P(("groups", "latent"), "hidden")
    one = P(("groups", "latent"))
    return jax.shard_map(
        local,
        mesh=mesh,
        in_specs=(both, P(("groups", "hidden")), both, one, both, P(None, ("groups", "latent")), both,
                  P("groups", None), P("groups"), P("groups")),
        out_specs=(one, both, both, one, P(None, ("groups", "latent"))),
        check_vma=False,
    )
```

```python
import math

import jax
import jax.numpy as jnp
from jax import lax
from jax.experimental import pallas as pl
from jax.experimental.pallas import tpu as pltpu
from jax.sharding import PartitionSpec as P

BLOCK = 32
EPS = 1e-06
F32, BF16 = jnp.float32, jnp.bfloat16


def swap(x):
    return lax.ppermute(x, "hidden", [(0, 1), (1, 0)])


def middle_out(owners):
    return sorted(range(owners), key=lambda i: (abs(4 * (i // 2) - owners + 2), i // 2, abs(2 * i - owners + 1)))


def outgoing(tokens, pool, dead_ids, row_ids, firsts, lat_dev):
    tok_dev, width = tokens.shape
    pool_dev, owners = pool.shape[0], firsts.shape[0]
    dead = dead_ids.shape[1]
    part = width // tok_dev

    def body(tokens_ref, pool_ref, dead_ref, row_ref, firsts_ref, out_ref, buffer, sems):
        copies = [
            pltpu.make_async_copy(tokens_ref, out_ref.at[dest, :, pl.ds(0, width)], sems.at[dest])
            for dest in range(owners)
        ]
        for copy in copies:
            copy.start()
        me = lax.axis_index("latent")
        first = firsts_ref[...]
        there = (dead_ref[...] >= first) & (dead_ref[...] < first + lat_dev)
        slot = lax.broadcasted_iota(jnp.int32, (pool_dev, dead), 0) + me * pool_dev
        goes = jnp.where(there, 1.0, 0.0).astype(BF16)
        lies = jnp.where(row_ref[...] == slot, 1.0, 0.0).astype(BF16)
        take = lax.dot_general(goes, lies, (((1,), (1,)), ((), ())), preferred_element_type=F32).astype(BF16)
        rows = jnp.dot(take, pool_ref[...], preferred_element_type=F32)
        for piece in range(tok_dev):
            buffer[:, piece, :] = rows[:, piece * part : (piece + 1) * part].astype(BF16)
        last = pltpu.make_async_copy(buffer, out_ref.at[:, :, pl.ds(width, part)], sems.at[owners])
        last.start()
        for copy in copies + [last]:
            copy.wait()

    in_vmem_spec = pl.BlockSpec(memory_space=pltpu.VMEM)
    return pl.pallas_call(
        body,
        out_shape=jax.ShapeDtypeStruct((owners, tok_dev, width + part), BF16),
        in_specs=[in_vmem_spec] * 5,
        out_specs=pl.BlockSpec(memory_space=pl.ANY),
        scratch_shapes=[pltpu.VMEM((owners, tok_dev, part), BF16), pltpu.SemaphoreType.DMA((owners + 1,))],
        name="outgoing",
    )(tokens, pool, dead_ids, row_ids, firsts)


def small(shape, dtype):
    return math.prod(shape) * jnp.dtype(dtype).itemsize <= 1 << 20


def in_vmem(*arrays):
    return [pltpu.with_memory_space_constraint(x, pltpu.VMEM) if small(x.shape, x.dtype) else x for x in arrays]


def resampled(summed, unit, place, w_enc, living, lat_dev):
    width = w_enc.shape[1]
    pieces = 4
    chunk = width // pieces

    def body(summed_ref, unit_ref, place_ref, enc_ref, out_ref, buffer, sems):
        first = width + lat_dev
        norms = summed_ref[0:1, first : first + lat_dev] + summed_ref[0:1, first + 2 * lat_dev : first + 3 * lat_dev]
        scale = 0.2 * (jnp.sum(norms, axis=1, keepdims=True) / living)
        dead = jnp.sum(place_ref[...].astype(F32), axis=1, keepdims=True) > 0.0
        copies = []
        for i in range(pieces):
            columns = slice(i * chunk, (i + 1) * chunk)
            rows = (scale * unit_ref[:, columns]).astype(BF16)
            placed = jnp.dot(place_ref[...], rows, preferred_element_type=F32)
            buffer[:, columns] = jnp.where(dead, placed, enc_ref[:, columns].astype(F32)).astype(BF16)
            copy = pltpu.make_async_copy(buffer.at[:, columns], out_ref.at[:, columns], sems.at[i])
            copy.start()
            copies.append(copy)
        for copy in copies:
            copy.wait()

    return pl.pallas_call(
        body,
        out_shape=jax.ShapeDtypeStruct(w_enc.shape, BF16),
        in_specs=[pl.BlockSpec(memory_space=pltpu.VMEM)] * 4,
        out_specs=pl.BlockSpec(memory_space=pl.ANY),
        scratch_shapes=[pltpu.VMEM(w_enc.shape, BF16), pltpu.SemaphoreType.DMA((pieces,))],
        name="resampled",
    )(*in_vmem(summed, unit, place, w_enc))


def encoded(own, peer, b_enc, mask, living, w_dec, owners):
    count, lat_dev = mask.shape
    width = w_dec.shape[1]
    tok_dev = count // owners
    pieces = 4
    chunk = width // pieces

    def body(own_ref, peer_ref, bias_ref, mask_ref, living_ref, dec_ref, out_ref, buffer, sems):
        total = own_ref[: count + 2, :] + peer_ref[: count + 2, :]
        codes = (jnp.maximum(total[:count] + bias_ref[...], 0.0) * mask_ref[...]).astype(BF16)
        copies = []

        def send(i, columns):
            copy = pltpu.make_async_copy(buffer.at[:, :, columns], out_ref.at[:, :, columns], sems.at[i])
            copy.start()
            copies.append(copy)

        for i in range(pieces):
            columns = slice(i * chunk, (i + 1) * chunk)
            part = jnp.dot(codes, dec_ref[:, columns], preferred_element_type=F32).astype(BF16)
            buffer[:, :, columns] = part.reshape(owners, tok_dev, chunk)
            send(i, columns)
        norms = jnp.sqrt(total[count : count + 2])
        alive = jnp.broadcast_to(norms[1:2] * living_ref[...], (count, lat_dev))
        side = jnp.concatenate([codes.astype(F32) * norms[0:1], alive], axis=1)
        high = side.astype(BF16)
        low = (side - high.astype(F32)).astype(BF16)
        buffer[:, :, width:] = jnp.concatenate([high, low], axis=1).reshape(owners, tok_dev, 4 * lat_dev)
        send(pieces, slice(width, width + 4 * lat_dev))
        for copy in copies:
            copy.wait()

    shape = (owners, tok_dev, width + 4 * lat_dev)
    return pl.pallas_call(
        body,
        out_shape=jax.ShapeDtypeStruct(shape, BF16),
        in_specs=[pl.BlockSpec(memory_space=pltpu.VMEM)] * 6,
        out_specs=pl.BlockSpec(memory_space=pl.ANY),
        scratch_shapes=[pltpu.VMEM(shape, BF16), pltpu.SemaphoreType.DMA((pieces + 1,))],
        name="encoded",
    )(*in_vmem(own, peer, b_enc, mask, living, w_dec))


def directions(got, b_dec, total, place, w_dec):
    owners, tok_dev, _ = got.shape
    lat_dev, width = w_dec.shape
    part = width // tok_dev
    pieces = 2
    chunk = part // pieces

    def column(row, size):
        rows, lanes = (lax.broadcasted_iota(jnp.int32, (size, row.shape[1]), i) for i in range(2))
        return jnp.sum(jnp.where(rows == lanes, row, 0.0), axis=1, keepdims=True)

    def body(got_ref, bias_ref, total_ref, place_ref, dec_ref, out_ref, unit_ref, buffer, sems):
        fresh_sq = column(total_ref[2:3, :], owners)
        if owners > lat_dev:
            fresh_sq = jnp.concatenate(
                [column(total_ref[2 + i : 3 + i, :], lat_dev) for i in range(owners // lat_dev)], axis=0)
        scale = lax.rsqrt(fresh_sq + EPS)
        again = lax.rsqrt(fresh_sq / (fresh_sq + EPS) + EPS)
        alive = lax.rsqrt(column(total_ref[0:1, :], lat_dev) + EPS)
        dead = jnp.sum(place_ref[...].astype(F32), axis=1, keepdims=True) > 0.0
        copies = []
        for i in range(tok_dev * pieces):
            columns = slice(i * chunk, (i + 1) * chunk)
            lanes = slice(width + i % pieces * chunk, width + (i % pieces + 1) * chunk)
            unit = (got_ref[:, i // pieces, lanes].astype(F32) - bias_ref[:, columns]) * scale
            unit_ref[:, columns] = unit
            placed = jnp.dot(place_ref[...], (unit * again).astype(BF16), preferred_element_type=F32)
            buffer[:, columns] = jnp.where(dead, placed, dec_ref[:, columns].astype(F32) * alive).astype(BF16)
            copy = pltpu.make_async_copy(buffer.at[:, columns], out_ref.at[:, columns], sems.at[i])
            copy.start()
            copies.append(copy)
        for copy in copies:
            copy.wait()

    make = pltpu.VMEM if small((owners, width), F32) else jax.ShapeDtypeStruct
    unit_shape = make((owners, width), F32)
    return pl.pallas_call(
        body,
        out_shape=(jax.ShapeDtypeStruct(w_dec.shape, BF16), unit_shape),
        in_specs=[pl.BlockSpec(memory_space=pltpu.VMEM)] * 5,
        out_specs=(pl.BlockSpec(memory_space=pl.ANY), pl.BlockSpec(memory_space=pltpu.VMEM)),
        scratch_shapes=[pltpu.VMEM(w_dec.shape, BF16), pltpu.SemaphoreType.DMA((tok_dev * pieces,))],
        cost_estimate=pl.CostEstimate(flops=20 * lat_dev * width, bytes_accessed=8 * lat_dev * width, transcendentals=0),
        name="directions",
    )(*in_vmem(got, b_dec, total, place, w_dec))


def local(tokens, b_dec, w_enc, b_enc, w_dec, bias_moments, pool, active_blocks, dead_ids, row_ids):
    lat_dev, width = w_enc.shape
    owners = lax.axis_size("latent")
    me = lax.axis_index("latent")
    tok_dev, pool_dev = tokens.shape[0], pool.shape[0]
    latents, count = lat_dev * owners, tok_dev * owners
    dead = dead_ids.shape[0]
    tiles = active_blocks.shape[0]
    part = width // tok_dev
    holder_of = row_ids // pool_dev
    order = middle_out(owners)
    everyone = jnp.array(order, jnp.int32)
    sent = outgoing(tokens, pool, dead_ids[None], row_ids[None], everyone[:, None] * lat_dev, lat_dev)
    got = lax.all_to_all(sent, "latent", 0, 0, axis_index_groups=[order])

    local_ids = me * lat_dev + jnp.arange(lat_dev, dtype=jnp.int32)
    dead_hit = dead_ids[None, :] == local_ids[:, None]
    is_dead = jnp.any(dead_hit, axis=1)
    place = lax.dot_general(
        dead_hit.astype(BF16), (holder_of[None, :] == everyone[:, None]).astype(BF16),
        (((1,), (1,)), ((), ())), preferred_element_type=F32).astype(BF16)
    keep = jnp.where(is_dead, 0.0, 1.0)
    new_b_enc = b_enc * keep
    new_moments = bias_moments * keep[None, :]
    row_tile = jnp.repeat(everyone, tok_dev) // (owners // tiles)
    my_block = local_ids // BLOCK
    listed = jnp.any(active_blocks[:, :, None] == my_block[None, None, :], axis=1).astype(F32)
    mask = jnp.zeros((count, lat_dev), F32)
    for tile in range(tiles):
        mask = jnp.where(row_tile[:, None] == tile, listed[tile][None, :], mask)
    dec_wide = w_dec.astype(F32)
    dec_part = jnp.sum(dec_wide * dec_wide, axis=1)
    enc_part = jnp.sum(jnp.square(w_enc.astype(F32)), axis=1)
    own_centered = tokens.astype(F32) - b_dec[None, :]
    input_part = jnp.sum(own_centered * own_centered, axis=1)
    centered = (got[:, :, :width].astype(F32) - b_dec[None, None, :]).astype(BF16).reshape(count, width)
    partial_pre = lax.dot_general(centered, w_enc, (((1,), (1,)), ((), ())), preferred_element_type=F32)
    fresh = got[:, :, width:].astype(F32) - b_dec.reshape(tok_dev, part)[None]
    tail = jnp.concatenate([jnp.sum(fresh * fresh, axis=(1, 2)), input_part])
    tail = jnp.pad(tail, (0, -tail.shape[0] % lat_dev)).reshape(-1, lat_dev)
    message = jnp.concatenate([partial_pre, dec_part[None], enc_part[None], tail], axis=0)
    peer = swap(message)
    sent = encoded(message, peer, b_enc[None], mask, keep[None], w_dec, owners)
    summed = lax.all_to_all(sent, "latent", 0, 0, axis_index_groups=[order])

    total = message[count:] + peer[count:]
    input_sum = total[2:].reshape(-1)[owners : owners + tok_dev]
    new_dec, unit = directions(got, b_dec[None], total, place, w_dec)
    summed, new_dec, unit = lax.optimization_barrier((summed, new_dec, unit))

    summed = jnp.sum(summed.astype(F32), axis=0)
    residual = own_centered - summed[:, :width]
    error_part = jnp.sum(jnp.square(residual).reshape(tok_dev, -1, 128), axis=1)
    error_peer = swap(error_part)
    new_enc = resampled(summed, unit, place, w_enc, latents - dead, lat_dev)
    error_peer, new_enc = lax.optimization_barrier((error_peer, new_enc))
    side = summed[:, width : width + lat_dev] + summed[:, width + 2 * lat_dev : width + 3 * lat_dev]
    penalty = jnp.sum(side, axis=1)
    error_sum = jnp.sum(error_part + error_peer, axis=1)
    full = width * lax.axis_size("hidden")
    losses = error_sum / full / (input_sum / full + EPS) + 5.0 * penalty / latents
    return losses, new_enc, new_dec, new_b_enc, new_moments


def solution(mesh):
    both = P(("groups", "latent"), "hidden")
    one = P(("groups", "latent"))
    return jax.shard_map(
        local,
        mesh=mesh,
        in_specs=(both, P(("groups", "hidden")), both, one, both, P(None, ("groups", "latent")), both,
                  P("groups", None), P("groups"), P("groups")),
        out_specs=(one, both, both, one, P(None, ("groups", "latent"))),
        check_vma=False,
    )
```

```python
import math

import jax
import jax.numpy as jnp
from jax import lax
from jax.experimental import pallas as pl
from jax.experimental.pallas import tpu as pltpu
from jax.sharding import PartitionSpec as P

BLOCK = 32
EPS = 1e-06
F32, BF16 = jnp.float32, jnp.bfloat16


def swap(x):
    return lax.ppermute(x, "hidden", [(0, 1), (1, 0)])


def middle_out(owners):
    return sorted(range(owners), key=lambda i: (abs(4 * (i // 2) - owners + 2), i // 2, abs(2 * i - owners + 1)))


def outgoing(tokens, pool, dead_ids, row_ids, firsts, lat_dev):
    tok_dev, width = tokens.shape
    pool_dev, owners = pool.shape[0], firsts.shape[0]
    dead = dead_ids.shape[1]
    part = width // tok_dev

    def body(tokens_ref, pool_ref, dead_ref, row_ref, firsts_ref, out_ref, buffer, sems):
        copies = [
            pltpu.make_async_copy(tokens_ref, out_ref.at[dest, :, pl.ds(0, width)], sems.at[dest])
            for dest in range(owners)
        ]
        for copy in copies:
            copy.start()
        me = lax.axis_index("latent")
        first = firsts_ref[...]
        there = (dead_ref[...] >= first) & (dead_ref[...] < first + lat_dev)
        slot = lax.broadcasted_iota(jnp.int32, (pool_dev, dead), 0) + me * pool_dev
        goes = jnp.where(there, 1.0, 0.0).astype(BF16)
        lies = jnp.where(row_ref[...] == slot, 1.0, 0.0).astype(BF16)
        take = lax.dot_general(goes, lies, (((1,), (1,)), ((), ())), preferred_element_type=F32).astype(BF16)
        rows = jnp.dot(take, pool_ref[...], preferred_element_type=F32)
        for piece in range(tok_dev):
            buffer[:, piece, :] = rows[:, piece * part : (piece + 1) * part].astype(BF16)
        last = pltpu.make_async_copy(buffer, out_ref.at[:, :, pl.ds(width, part)], sems.at[owners])
        last.start()
        for copy in copies + [last]:
            copy.wait()

    in_vmem_spec = pl.BlockSpec(memory_space=pltpu.VMEM)
    return pl.pallas_call(
        body,
        out_shape=jax.ShapeDtypeStruct((owners, tok_dev, width + part), BF16),
        in_specs=[in_vmem_spec] * 5,
        out_specs=pl.BlockSpec(memory_space=pl.ANY),
        scratch_shapes=[pltpu.VMEM((owners, tok_dev, part), BF16), pltpu.SemaphoreType.DMA((owners + 1,))],
        name="outgoing",
    )(tokens, pool, dead_ids, row_ids, firsts)


def small(shape, dtype):
    return math.prod(shape) * jnp.dtype(dtype).itemsize <= 1 << 20


def in_vmem(*arrays):
    return [pltpu.with_memory_space_constraint(x, pltpu.VMEM) if small(x.shape, x.dtype) else x for x in arrays]


def encoded(own, peer, b_enc, mask, living, w_dec, owners):
    count, lat_dev = mask.shape
    width = w_dec.shape[1]
    tok_dev = count // owners
    pieces = 4
    chunk = width // pieces

    def body(own_ref, peer_ref, bias_ref, mask_ref, living_ref, dec_ref, out_ref):
        total = own_ref[: count + 2, :] + peer_ref[: count + 2, :]
        codes = (jnp.maximum(total[:count] + bias_ref[...], 0.0) * mask_ref[...]).astype(BF16)
        for i in range(pieces):
            columns = slice(i * chunk, (i + 1) * chunk)
            part = jnp.dot(codes, dec_ref[:, columns], preferred_element_type=F32).astype(BF16)
            out_ref[:, :, columns] = part.reshape(owners, tok_dev, chunk)
        norms = jnp.sqrt(total[count : count + 2])
        alive = jnp.broadcast_to(norms[1:2] * living_ref[...], (count, lat_dev))
        side = jnp.concatenate([codes.astype(F32) * norms[0:1], alive], axis=1)
        high = side.astype(BF16)
        low = (side - high.astype(F32)).astype(BF16)
        out_ref[:, :, width:] = jnp.concatenate([high, low], axis=1).reshape(owners, tok_dev, 4 * lat_dev)

    shape = (owners, tok_dev, width + 4 * lat_dev)
    return pl.pallas_call(
        body,
        out_shape=(pltpu.VMEM if small(shape, BF16) else jax.ShapeDtypeStruct)(shape, BF16),
        in_specs=[pl.BlockSpec(memory_space=pltpu.VMEM)] * 6,
        out_specs=pl.BlockSpec(memory_space=pltpu.VMEM),
        name="encoded",
    )(*in_vmem(own, peer, b_enc, mask, living, w_dec))


def finished(summed, got, b_dec, total, place, w_enc, w_dec, living):
    owners, tok_dev, _ = got.shape
    lat_dev, width = w_dec.shape
    part = width // tok_dev
    pieces = 2
    chunk = part // pieces
    steps = tok_dev * pieces

    def column(row, size):
        rows, lanes = (lax.broadcasted_iota(jnp.int32, (size, row.shape[1]), i) for i in range(2))
        return jnp.sum(jnp.where(rows == lanes, row, 0.0), axis=1, keepdims=True)

    def body(summed_ref, got_ref, bias_ref, total_ref, place_ref, enc_ref, dec_ref, new_enc_ref, new_dec_ref,
             enc_buffer, dec_buffer, sems):
        first = width + lat_dev
        norms = summed_ref[0:1, first : first + lat_dev] + summed_ref[0:1, first + 2 * lat_dev : first + 3 * lat_dev]
        level = 0.2 * (jnp.sum(norms, axis=1, keepdims=True) / living)
        lanes = min(owners, lat_dev)
        fresh_sq = jnp.concatenate(
            [column(total_ref[2 + i : 3 + i, :], lanes) for i in range(owners // lanes)], axis=0)
        scale = lax.rsqrt(fresh_sq + EPS)
        again = lax.rsqrt(fresh_sq / (fresh_sq + EPS) + EPS)
        alive = lax.rsqrt(column(total_ref[0:1, :], lat_dev) + EPS)
        dead = jnp.sum(place_ref[...].astype(F32), axis=1, keepdims=True) > 0.0
        copies = []

        def send(buffer, out_ref, columns):
            copy = pltpu.make_async_copy(buffer.at[:, columns], out_ref.at[:, columns], sems.at[len(copies)])
            copy.start()
            copies.append(copy)

        for i in range(steps):
            columns = slice(i * chunk, (i + 1) * chunk)
            lane = width + i % pieces * chunk
            unit = (got_ref[:, i // pieces, lane : lane + chunk].astype(F32) - bias_ref[:, columns]) * scale
            placed = jnp.dot(place_ref[...], (level * unit).astype(BF16), preferred_element_type=F32)
            enc_buffer[:, columns] = jnp.where(dead, placed, enc_ref[:, columns].astype(F32)).astype(BF16)
            send(enc_buffer, new_enc_ref, columns)
            placed = jnp.dot(place_ref[...], (unit * again).astype(BF16), preferred_element_type=F32)
            dec_buffer[:, columns] = jnp.where(dead, placed, dec_ref[:, columns].astype(F32) * alive).astype(BF16)
            send(dec_buffer, new_dec_ref, columns)
        for copy in copies:
            copy.wait()

    like = jax.ShapeDtypeStruct(w_dec.shape, BF16)
    return pl.pallas_call(
        body,
        out_shape=(like, like),
        in_specs=[pl.BlockSpec(memory_space=pltpu.VMEM)] * 7,
        out_specs=[pl.BlockSpec(memory_space=pl.ANY)] * 2,
        scratch_shapes=[pltpu.VMEM(w_dec.shape, BF16)] * 2 + [pltpu.SemaphoreType.DMA((2 * steps,))],
        name="finished",
    )(*in_vmem(summed, got, b_dec, total, place, w_enc, w_dec))


def local(tokens, b_dec, w_enc, b_enc, w_dec, bias_moments, pool, active_blocks, dead_ids, row_ids):
    lat_dev, width = w_enc.shape
    owners = lax.axis_size("latent")
    me = lax.axis_index("latent")
    tok_dev, pool_dev = tokens.shape[0], pool.shape[0]
    latents, count = lat_dev * owners, tok_dev * owners
    dead = dead_ids.shape[0]
    tiles = active_blocks.shape[0]
    part = width // tok_dev
    holder_of = row_ids // pool_dev
    order = middle_out(owners)
    everyone = jnp.array(order, jnp.int32)
    sent = outgoing(tokens, pool, dead_ids[None], row_ids[None], everyone[:, None] * lat_dev, lat_dev)
    got = lax.all_to_all(sent, "latent", 0, 0, axis_index_groups=[order])

    local_ids = me * lat_dev + jnp.arange(lat_dev, dtype=jnp.int32)
    dead_hit = dead_ids[None, :] == local_ids[:, None]
    is_dead = jnp.any(dead_hit, axis=1)
    place = lax.dot_general(
        dead_hit.astype(BF16), (holder_of[None, :] == everyone[:, None]).astype(BF16),
        (((1,), (1,)), ((), ())), preferred_element_type=F32).astype(BF16)
    keep = jnp.where(is_dead, 0.0, 1.0)
    new_b_enc = b_enc * keep
    new_moments = bias_moments * keep[None, :]
    row_tile = jnp.repeat(everyone, tok_dev) // (owners // tiles)
    my_block = local_ids // BLOCK
    listed = jnp.any(active_blocks[:, :, None] == my_block[None, None, :], axis=1).astype(F32)
    mask = jnp.zeros((count, lat_dev), F32)
    for tile in range(tiles):
        mask = jnp.where(row_tile[:, None] == tile, listed[tile][None, :], mask)
    dec_wide = w_dec.astype(F32)
    dec_part = jnp.sum(dec_wide * dec_wide, axis=1)
    enc_part = jnp.sum(jnp.square(w_enc.astype(F32)), axis=1)
    own_centered = tokens.astype(F32) - b_dec[None, :]
    input_part = jnp.sum(own_centered * own_centered, axis=1)
    centered = (got[:, :, :width].astype(F32) - b_dec[None, None, :]).astype(BF16).reshape(count, width)
    partial_pre = lax.dot_general(centered, w_enc, (((1,), (1,)), ((), ())), preferred_element_type=F32)
    fresh = got[:, :, width:].astype(F32) - b_dec.reshape(tok_dev, part)[None]
    tail = jnp.concatenate([jnp.sum(fresh * fresh, axis=(1, 2)), input_part])
    tail = jnp.pad(tail, (0, -tail.shape[0] % lat_dev)).reshape(-1, lat_dev)
    message = jnp.concatenate([partial_pre, dec_part[None], enc_part[None], tail], axis=0)
    peer, new_b_enc, new_moments, place = lax.optimization_barrier((swap(message), new_b_enc, new_moments, place))
    sent = encoded(message, peer, b_enc[None], mask, keep[None], w_dec, owners)
    summed = lax.all_to_all(sent, "latent", 0, 0, axis_index_groups=[order])
    summed, got, message, peer = lax.optimization_barrier((summed, got, message, peer))
    total = message[count:] + peer[count:]
    input_sum = total[2:].reshape(-1)[owners : owners + tok_dev]
    summed = jnp.sum(summed.astype(F32), axis=0)
    residual = own_centered - summed[:, :width]
    error_part = jnp.sum(jnp.square(residual).reshape(tok_dev, -1, 128), axis=1)
    error_peer = swap(error_part)
    new_enc, new_dec = finished(summed, got, b_dec[None], total, place, w_enc, w_dec, latents - dead)
    error_peer, new_enc, new_dec = lax.optimization_barrier((error_peer, new_enc, new_dec))
    side = summed[:, width : width + lat_dev] + summed[:, width + 2 * lat_dev : width + 3 * lat_dev]
    penalty = jnp.sum(side, axis=1)
    error_sum = jnp.sum(error_part + error_peer, axis=1)
    full = width * lax.axis_size("hidden")
    losses = error_sum / full / (input_sum / full + EPS) + 5.0 * penalty / latents
    return losses, new_enc, new_dec, new_b_enc, new_moments


def solution(mesh):
    both = P(("groups", "latent"), "hidden")
    one = P(("groups", "latent"))
    return jax.shard_map(
        local,
        mesh=mesh,
        in_specs=(both, P(("groups", "hidden")), both, one, both, P(None, ("groups", "latent")), both,
                  P("groups", None), P("groups"), P("groups")),
        out_specs=(one, both, both, one, P(None, ("groups", "latent"))),
        check_vma=False,
    )
```

```python
import math

import jax
import jax.numpy as jnp
from jax import lax
from jax.experimental import pallas as pl
from jax.experimental.pallas import tpu as pltpu
from jax.sharding import PartitionSpec as P

BLOCK = 32
EPS = 1e-06
F32, BF16 = jnp.float32, jnp.bfloat16


def swap(x):
    return lax.ppermute(x, "hidden", [(0, 1), (1, 0)])


def middle_out(owners):
    return sorted(range(owners), key=lambda i: (abs(4 * (i // 2) - owners + 2), i // 2, abs(2 * i - owners + 1)))


def small(shape, dtype):
    return math.prod(shape) * jnp.dtype(dtype).itemsize <= 1 << 20


def in_vmem(*arrays):
    return [pltpu.with_memory_space_constraint(x, pltpu.VMEM) if small(x.shape, x.dtype) else x for x in arrays]


def pinned(shape, dtype):
    return (pltpu.VMEM if small(shape, dtype) else jax.ShapeDtypeStruct)(shape, dtype)


def prepared(tokens, pool, dead_ids, row_ids, order, active_blocks, b_enc, moments, b_dec, w_enc, w_dec):
    tok_dev, width = tokens.shape
    lat_dev = w_enc.shape[0]
    pool_dev, owners = pool.shape[0], order.shape[0]
    dead, tiles = dead_ids.shape[1], active_blocks.shape[0]
    part = width // tok_dev
    members = middle_out(owners)

    def body(*refs):
        sources, (tokens_ref, pool_ref, dead_ref, row_ref, order_ref, active_ref, moments_ref) = refs[:11], refs[23:30]
        out_ref, mask_ref, place_ref, living_ref, centered_ref, squares_ref = refs[11:17]
        bias_ref, enc_bias_ref, enc_ref, dec_ref, new_bias_ref, new_moments_ref = refs[17:23]
        bias_buffer, moments_buffer, sems = refs[30:]
        targets = (tokens_ref, pool_ref, dead_ref, row_ref, order_ref, active_ref, moments_ref,
                   bias_ref, enc_bias_ref, enc_ref, dec_ref)
        copies = [pltpu.make_async_copy(x, y, sems.at[i]) for i, (x, y) in enumerate(zip(sources, targets))]
        for copy in copies:
            copy.start()
        for copy in copies[:9]:
            copy.wait()
        me = lax.axis_index("latent")
        first = order_ref[...] * lat_dev
        there = (dead_ref[...] >= first) & (dead_ref[...] < first + lat_dev)
        slot = lax.broadcasted_iota(jnp.int32, (pool_dev, dead), 0) + me * pool_dev
        goes = jnp.where(there, 1.0, 0.0).astype(BF16)
        lies = jnp.where(row_ref[...] == slot, 1.0, 0.0).astype(BF16)
        take = lax.dot_general(goes, lies, (((1,), (1,)), ((), ())), preferred_element_type=F32).astype(BF16)
        rows = jnp.dot(take, pool_ref[...], preferred_element_type=F32)
        for dest in range(owners):
            out_ref[dest, :, :width] = tokens_ref[...]
        for piece in range(tok_dev):
            out_ref[:, piece, width:] = rows[:, piece * part : (piece + 1) * part].astype(BF16)

        ids = lax.broadcasted_iota(jnp.int32, (lat_dev, dead), 0) + me * lat_dev
        hit = jnp.where(dead_ref[...] == ids, 1.0, 0.0).astype(BF16)
        held = order_ref[...] * pool_dev
        source = jnp.where((row_ref[...] >= held) & (row_ref[...] < held + pool_dev), 1.0, 0.0).astype(BF16)
        across = (((1,), (1,)), ((), ()))
        place_ref[...] = lax.dot_general(hit, source, across, preferred_element_type=F32).astype(BF16)
        hits = lax.dot_general(jnp.ones((8, dead), BF16), hit, across, preferred_element_type=F32)
        living = jnp.where(hits[0:1] > 0.0, 0.0, 1.0)
        living_ref[...] = living
        bias_buffer[...] = enc_bias_ref[...] * living
        moments_buffer[...] = moments_ref[...] * living
        results = [pltpu.make_async_copy(bias_buffer, new_bias_ref, sems.at[11]),
                   pltpu.make_async_copy(moments_buffer, new_moments_ref, sems.at[12])]
        for copy in results:
            copy.start()
        block = lax.broadcasted_iota(jnp.int32, (tiles, lat_dev), 1) // BLOCK
        listed = jnp.zeros((tiles, lat_dev), F32)
        for i in range(lat_dev // BLOCK):
            here = jnp.where(active_ref[...] == me * (lat_dev // BLOCK) + i, 1.0, 0.0)
            listed = jnp.where(block == i, jnp.max(here, axis=1, keepdims=True), listed)
        for i, member in enumerate(members):
            tile = member * tiles // owners
            mask_ref[i * tok_dev : (i + 1) * tok_dev, :] = jnp.broadcast_to(listed[tile : tile + 1], (tok_dev, lat_dev))
        centered = tokens_ref[...].astype(F32) - bias_ref[...]
        centered_ref[...] = centered
        squares = jnp.zeros((tok_dev, lat_dev), F32)
        for i in range(width // lat_dev):
            lanes = centered[:, i * lat_dev : (i + 1) * lat_dev]
            squares = squares + lanes * lanes
        squares_ref[...] = squares
        for copy in copies[9:] + results:
            copy.wait()

    given = (tokens, pool, dead_ids, row_ids, order, active_blocks, moments, b_dec, b_enc, w_enc, w_dec)
    on_device, small_results = pl.BlockSpec(memory_space=pltpu.VMEM), (b_enc, moments)
    return pl.pallas_call(
        body,
        out_shape=(
            pinned((owners, tok_dev, width + part), BF16),
            pinned((owners * tok_dev, lat_dev), F32),
            pinned((lat_dev, owners), BF16),
            pinned((1, lat_dev), F32),
            pinned((tok_dev, width), F32),
            pinned((tok_dev, lat_dev), F32),
            *(pinned(x.shape, x.dtype) for x in given[7:]),
            *(jax.ShapeDtypeStruct(x.shape, x.dtype) for x in small_results),
        ),
        in_specs=[pl.BlockSpec(memory_space=pl.ANY)] * 11,
        out_specs=[on_device] * 10 + [pl.BlockSpec(memory_space=pl.ANY)] * 2,
        scratch_shapes=[pltpu.VMEM(x.shape, x.dtype) for x in given[:7] + small_results]
        + [pltpu.SemaphoreType.DMA((13,))],
        name="prepared",
    )(*given)


def compared(got, b_dec, squares, w_enc, w_dec):
    owners, tok_dev, _ = got.shape
    lat_dev, width = w_enc.shape
    count, part = owners * tok_dev, width // tok_dev
    pieces = 4
    chunk = width // pieces
    lanes = min(owners, lat_dev)
    extra = owners // lanes

    def spread(column):
        size = column.shape[0]
        down, along = (lax.broadcasted_iota(jnp.int32, (size, lat_dev), i) for i in range(2))
        return jnp.sum(jnp.where(down == along, column, 0.0), axis=0, keepdims=True)

    def folded(x):
        total = x[:, :lat_dev] * x[:, :lat_dev]
        for i in range(1, x.shape[1] // lat_dev):
            piece = x[:, i * lat_dev : (i + 1) * lat_dev]
            total = total + piece * piece
        return total

    def body(got_ref, bias_ref, squares_ref, enc_ref, dec_ref, out_ref):
        pre = jnp.zeros((count, lat_dev), F32)
        enc_sq = jnp.zeros((lat_dev, lat_dev), F32)
        dec_sq = jnp.zeros((lat_dev, lat_dev), F32)
        for i in range(pieces):
            columns = slice(i * chunk, (i + 1) * chunk)
            rows = got_ref[:, :, columns].reshape(count, chunk).astype(F32)
            centered = (rows - bias_ref[:, columns]).astype(BF16)
            pre = pre + lax.dot_general(
                centered, enc_ref[:, columns], (((1,), (1,)), ((), ())), preferred_element_type=F32)
            enc_sq = enc_sq + folded(enc_ref[:, columns].astype(F32))
            dec_sq = dec_sq + folded(dec_ref[:, columns].astype(F32))
        fresh = jnp.zeros((owners, lat_dev), F32)
        for i in range(tok_dev):
            fresh = fresh + folded(got_ref[:, i, width:].astype(F32) - bias_ref[:, i * part : (i + 1) * part])
        fresh = jnp.sum(fresh, axis=1, keepdims=True)
        out_ref[:count, :] = pre
        out_ref[count : count + 1, :] = spread(jnp.sum(dec_sq, axis=1, keepdims=True))
        out_ref[count + 1 : count + 2, :] = spread(jnp.sum(enc_sq, axis=1, keepdims=True))
        for i in range(extra):
            out_ref[count + 2 + i : count + 3 + i, :] = spread(fresh[i * lanes : (i + 1) * lanes])
        out_ref[count + 2 + extra :, :] = squares_ref[...]

    return pl.pallas_call(
        body,
        out_shape=pinned((count + 2 + extra + tok_dev, lat_dev), F32),
        in_specs=[pl.BlockSpec(memory_space=pltpu.VMEM)] * 5,
        out_specs=pl.BlockSpec(memory_space=pltpu.VMEM),
        name="compared",
    )(*in_vmem(got, b_dec, squares, w_enc, w_dec))


def encoded(own, peer, b_enc, mask, living, w_enc, w_dec, owners):
    count, lat_dev = mask.shape
    width = w_dec.shape[1]
    tok_dev = count // owners
    pieces = 4
    chunk = width // pieces

    def body(own_ref, peer_ref, bias_ref, mask_ref, living_ref, _, dec_ref, out_ref):
        total = own_ref[: count + 2, :] + peer_ref[: count + 2, :]
        codes = (jnp.maximum(total[:count] + bias_ref[...], 0.0) * mask_ref[...]).astype(BF16)
        for i in range(pieces):
            columns = slice(i * chunk, (i + 1) * chunk)
            part = jnp.dot(codes, dec_ref[:, columns], preferred_element_type=F32).astype(BF16)
            out_ref[:, :, columns] = part.reshape(owners, tok_dev, chunk)
        norms = jnp.sqrt(total[count : count + 2])
        alive = jnp.broadcast_to(norms[1:2] * living_ref[...], (count, lat_dev))
        side = jnp.concatenate([codes.astype(F32) * norms[0:1], alive], axis=1)
        high = side.astype(BF16)
        low = (side - high.astype(F32)).astype(BF16)
        out_ref[:, :, width:] = jnp.concatenate([high, low], axis=1).reshape(owners, tok_dev, 4 * lat_dev)

    shape = (owners, tok_dev, width + 4 * lat_dev)
    return pl.pallas_call(
        body,
        out_shape=(pltpu.VMEM if small(shape, BF16) else jax.ShapeDtypeStruct)(shape, BF16),
        in_specs=[pl.BlockSpec(memory_space=pltpu.VMEM)] * 7,
        out_specs=pl.BlockSpec(memory_space=pltpu.VMEM),
        name="encoded",
    )(*in_vmem(own, peer, b_enc, mask, living, w_enc, w_dec))


def finished(summed, got, b_dec, total, place, w_enc, w_dec, living):
    owners, tok_dev, _ = got.shape
    lat_dev, width = w_dec.shape
    part = width // tok_dev
    pieces = 2
    chunk = part // pieces
    steps = tok_dev * pieces

    def column(row, size):
        rows, lanes = (lax.broadcasted_iota(jnp.int32, (size, row.shape[1]), i) for i in range(2))
        return jnp.sum(jnp.where(rows == lanes, row, 0.0), axis=1, keepdims=True)

    def body(summed_ref, got_ref, bias_ref, total_ref, place_ref, enc_ref, dec_ref, new_enc_ref, new_dec_ref,
             enc_buffer, dec_buffer, sems):
        first = width + lat_dev
        norms = summed_ref[0:1, first : first + lat_dev] + summed_ref[0:1, first + 2 * lat_dev : first + 3 * lat_dev]
        level = 0.2 * (jnp.sum(norms, axis=1, keepdims=True) / living)
        lanes = min(owners, lat_dev)
        fresh_sq = jnp.concatenate(
            [column(total_ref[2 + i : 3 + i, :], lanes) for i in range(owners // lanes)], axis=0)
        scale = lax.rsqrt(fresh_sq + EPS)
        again = lax.rsqrt(fresh_sq / (fresh_sq + EPS) + EPS)
        alive = lax.rsqrt(column(total_ref[0:1, :], lat_dev) + EPS)
        dead = jnp.sum(place_ref[...].astype(F32), axis=1, keepdims=True) > 0.0
        copies = []

        def send(buffer, out_ref, columns):
            copy = pltpu.make_async_copy(buffer.at[:, columns], out_ref.at[:, columns], sems.at[len(copies)])
            copy.start()
            copies.append(copy)

        for i in range(steps):
            columns = slice(i * chunk, (i + 1) * chunk)
            lane = width + i % pieces * chunk
            unit = (got_ref[:, i // pieces, lane : lane + chunk].astype(F32) - bias_ref[:, columns]) * scale
            placed = jnp.dot(place_ref[...], (level * unit).astype(BF16), preferred_element_type=F32)
            enc_buffer[:, columns] = jnp.where(dead, placed, enc_ref[:, columns].astype(F32)).astype(BF16)
            send(enc_buffer, new_enc_ref, columns)
            placed = jnp.dot(place_ref[...], (unit * again).astype(BF16), preferred_element_type=F32)
            dec_buffer[:, columns] = jnp.where(dead, placed, dec_ref[:, columns].astype(F32) * alive).astype(BF16)
            send(dec_buffer, new_dec_ref, columns)
        for copy in copies:
            copy.wait()

    like = jax.ShapeDtypeStruct(w_dec.shape, BF16)
    return pl.pallas_call(
        body,
        out_shape=(like, like),
        in_specs=[pl.BlockSpec(memory_space=pltpu.VMEM)] * 7,
        out_specs=[pl.BlockSpec(memory_space=pl.ANY)] * 2,
        scratch_shapes=[pltpu.VMEM(w_dec.shape, BF16)] * 2 + [pltpu.SemaphoreType.DMA((2 * steps,))],
        name="finished",
    )(*in_vmem(summed, got, b_dec, total, place, w_enc, w_dec))


def local(tokens, b_dec, w_enc, b_enc, w_dec, bias_moments, pool, active_blocks, dead_ids, row_ids):
    lat_dev, width = w_enc.shape
    owners = lax.axis_size("latent")
    tok_dev = tokens.shape[0]
    latents, count = lat_dev * owners, tok_dev * owners
    dead = dead_ids.shape[0]
    order = middle_out(owners)
    members = jnp.array(order, jnp.int32)[:, None]

    sent, mask, place, living, centered, squares, b_dec, b_enc, w_enc, w_dec, new_b_enc, new_moments = prepared(
        tokens, pool, dead_ids[None], row_ids[None], members, active_blocks, b_enc[None], bias_moments, b_dec[None],
        w_enc, w_dec)
    got = lax.all_to_all(sent, "latent", 0, 0, axis_index_groups=[order])
    message = compared(got, b_dec, squares, w_enc, w_dec)
    peer = swap(message)
    sent = encoded(message, peer, b_enc, mask, living, w_enc, w_dec, owners)
    summed = lax.all_to_all(sent, "latent", 0, 0, axis_index_groups=[order])
    summed, got, message, peer = lax.optimization_barrier((summed, got, message, peer))
    total = message[count:] + peer[count:]
    input_sum = jnp.sum(total[-tok_dev:], axis=1)
    summed = jnp.sum(summed.astype(F32), axis=0)
    residual = centered - summed[:, :width]
    error_part = jnp.sum(jnp.square(residual).reshape(tok_dev, -1, 128), axis=1)
    error_peer = swap(error_part)
    new_enc, new_dec = finished(summed, got, b_dec, total, place, w_enc, w_dec, latents - dead)
    error_peer, new_enc, new_dec = lax.optimization_barrier((error_peer, new_enc, new_dec))
    side = summed[:, width : width + lat_dev] + summed[:, width + 2 * lat_dev : width + 3 * lat_dev]
    penalty = jnp.sum(side, axis=1)
    error_sum = jnp.sum(error_part + error_peer, axis=1)
    full = width * lax.axis_size("hidden")
    losses = error_sum / full / (input_sum / full + EPS) + 5.0 * penalty / latents
    return losses, new_enc, new_dec, new_b_enc[0], new_moments


def solution(mesh):
    both = P(("groups", "latent"), "hidden")
    one = P(("groups", "latent"))
    return jax.shard_map(
        local,
        mesh=mesh,
        in_specs=(both, P(("groups", "hidden")), both, one, both, P(None, ("groups", "latent")), both,
                  P("groups", None), P("groups"), P("groups")),
        out_specs=(one, both, both, one, P(None, ("groups", "latent"))),
        check_vma=False,
    )
```

```python
import math

import jax
import jax.numpy as jnp
from jax import lax
from jax.experimental import pallas as pl
from jax.experimental.pallas import tpu as pltpu
from jax.sharding import PartitionSpec as P

BLOCK = 32
EPS = 1e-06
F32, BF16 = jnp.float32, jnp.bfloat16


def swap(x):
    return lax.ppermute(x, "hidden", [(0, 1), (1, 0)])


def middle_out(owners):
    return sorted(range(owners), key=lambda i: (abs(4 * (i // 2) - owners + 2), i // 2, abs(2 * i - owners + 1)))


def small(shape, dtype):
    return math.prod(shape) * jnp.dtype(dtype).itemsize <= 1 << 20


def in_vmem(*arrays):
    return [pltpu.with_memory_space_constraint(x, pltpu.VMEM) if small(x.shape, x.dtype) else x for x in arrays]


def pinned(shape, dtype):
    return (pltpu.VMEM if small(shape, dtype) else jax.ShapeDtypeStruct)(shape, dtype)


def prepared(tokens, pool, dead_ids, row_ids, order, active_blocks, b_enc, moments, b_dec, w_enc, w_dec):
    tok_dev, width = tokens.shape
    lat_dev = w_enc.shape[0]
    pool_dev, owners = pool.shape[0], order.shape[0]
    dead, tiles = dead_ids.shape[1], active_blocks.shape[0]
    part = width // tok_dev
    members = middle_out(owners)

    def body(*refs):
        sources, (tokens_ref, pool_ref, dead_ref, row_ref, order_ref, active_ref, moments_ref) = refs[:11], refs[23:30]
        out_ref, mask_ref, place_ref, living_ref, centered_ref, squares_ref = refs[11:17]
        bias_ref, enc_bias_ref, enc_ref, dec_ref, new_bias_ref, new_moments_ref = refs[17:23]
        bias_buffer, moments_buffer, sems = refs[30:]
        targets = (tokens_ref, pool_ref, dead_ref, row_ref, order_ref, active_ref, moments_ref,
                   bias_ref, enc_bias_ref, enc_ref, dec_ref)
        copies = [pltpu.make_async_copy(x, y, sems.at[i]) for i, (x, y) in enumerate(zip(sources, targets))]
        for copy in copies:
            copy.start()
        for copy in copies[:9]:
            copy.wait()
        me = lax.axis_index("latent")
        first = order_ref[...] * lat_dev
        there = (dead_ref[...] >= first) & (dead_ref[...] < first + lat_dev)
        slot = lax.broadcasted_iota(jnp.int32, (pool_dev, dead), 0) + me * pool_dev
        goes = jnp.where(there, 1.0, 0.0).astype(BF16)
        lies = jnp.where(row_ref[...] == slot, 1.0, 0.0).astype(BF16)
        take = lax.dot_general(goes, lies, (((1,), (1,)), ((), ())), preferred_element_type=F32).astype(BF16)
        rows = jnp.dot(take, pool_ref[...], preferred_element_type=F32)
        for dest in range(owners):
            out_ref[dest, :, :width] = tokens_ref[...]
        for piece in range(tok_dev):
            out_ref[:, piece, width:] = rows[:, piece * part : (piece + 1) * part].astype(BF16)

        ids = lax.broadcasted_iota(jnp.int32, (lat_dev, dead), 0) + me * lat_dev
        hit = jnp.where(dead_ref[...] == ids, 1.0, 0.0).astype(BF16)
        held = order_ref[...] * pool_dev
        source = jnp.where((row_ref[...] >= held) & (row_ref[...] < held + pool_dev), 1.0, 0.0).astype(BF16)
        across = (((1,), (1,)), ((), ()))
        place_ref[...] = lax.dot_general(hit, source, across, preferred_element_type=F32).astype(BF16)
        hits = lax.dot_general(jnp.ones((8, dead), BF16), hit, across, preferred_element_type=F32)
        living = jnp.where(hits[0:1] > 0.0, 0.0, 1.0)
        living_ref[...] = living
        bias_buffer[...] = enc_bias_ref[...] * living
        moments_buffer[...] = moments_ref[...] * living
        results = [pltpu.make_async_copy(bias_buffer, new_bias_ref, sems.at[11]),
                   pltpu.make_async_copy(moments_buffer, new_moments_ref, sems.at[12])]
        for copy in results:
            copy.start()
        block = lax.broadcasted_iota(jnp.int32, (tiles, lat_dev), 1) // BLOCK
        listed = jnp.zeros((tiles, lat_dev), F32)
        for i in range(lat_dev // BLOCK):
            here = jnp.where(active_ref[...] == me * (lat_dev // BLOCK) + i, 1.0, 0.0)
            listed = jnp.where(block == i, jnp.max(here, axis=1, keepdims=True), listed)
        for i, member in enumerate(members):
            tile = member * tiles // owners
            mask_ref[i * tok_dev : (i + 1) * tok_dev, :] = jnp.broadcast_to(listed[tile : tile + 1], (tok_dev, lat_dev))
        centered = tokens_ref[...].astype(F32) - bias_ref[...]
        centered_ref[...] = centered
        squares = jnp.zeros((tok_dev, lat_dev), F32)
        for i in range(width // lat_dev):
            lanes = centered[:, i * lat_dev : (i + 1) * lat_dev]
            squares = squares + lanes * lanes
        squares_ref[...] = squares
        for copy in copies[9:] + results:
            copy.wait()

    given = (tokens, pool, dead_ids, row_ids, order, active_blocks, moments, b_dec, b_enc, w_enc, w_dec)
    on_device, small_results = pl.BlockSpec(memory_space=pltpu.VMEM), (b_enc, moments)
    return pl.pallas_call(
        body,
        out_shape=(
            pinned((owners, tok_dev, width + part), BF16),
            pinned((owners * tok_dev, lat_dev), F32),
            pinned((lat_dev, owners), BF16),
            pinned((1, lat_dev), F32),
            pinned((tok_dev, width), F32),
            pinned((tok_dev, lat_dev), F32),
            *(pinned(x.shape, x.dtype) for x in given[7:]),
            *(jax.ShapeDtypeStruct(x.shape, x.dtype) for x in small_results),
        ),
        in_specs=[pl.BlockSpec(memory_space=pl.ANY)] * 11,
        out_specs=[on_device] * 10 + [pl.BlockSpec(memory_space=pl.ANY)] * 2,
        scratch_shapes=[pltpu.VMEM(x.shape, x.dtype) for x in given[:7] + small_results]
        + [pltpu.SemaphoreType.DMA((13,))],
        name="prepared",
    )(*given)


def compared(got, b_dec, squares, w_enc, w_dec):
    owners, tok_dev, _ = got.shape
    lat_dev, width = w_enc.shape
    count, part = owners * tok_dev, width // tok_dev
    pieces = 4
    chunk = width // pieces
    lanes = min(owners, lat_dev)
    extra = owners // lanes

    def spread(column):
        size = column.shape[0]
        down, along = (lax.broadcasted_iota(jnp.int32, (size, lat_dev), i) for i in range(2))
        return jnp.sum(jnp.where(down == along, column, 0.0), axis=0, keepdims=True)

    def folded(x):
        total = x[:, :lat_dev] * x[:, :lat_dev]
        for i in range(1, x.shape[1] // lat_dev):
            piece = x[:, i * lat_dev : (i + 1) * lat_dev]
            total = total + piece * piece
        return total

    def body(got_ref, bias_ref, squares_ref, enc_ref, dec_ref, out_ref):
        pre = jnp.zeros((count, lat_dev), F32)
        enc_sq = jnp.zeros((lat_dev, lat_dev), F32)
        dec_sq = jnp.zeros((lat_dev, lat_dev), F32)
        for i in range(pieces):
            columns = slice(i * chunk, (i + 1) * chunk)
            rows = got_ref[:, :, columns].reshape(count, chunk).astype(F32)
            centered = (rows - bias_ref[:, columns]).astype(BF16)
            pre = pre + lax.dot_general(
                centered, enc_ref[:, columns], (((1,), (1,)), ((), ())), preferred_element_type=F32)
            enc_sq = enc_sq + folded(enc_ref[:, columns].astype(F32))
            dec_sq = dec_sq + folded(dec_ref[:, columns].astype(F32))
        fresh = jnp.zeros((owners, lat_dev), F32)
        for i in range(tok_dev):
            fresh = fresh + folded(got_ref[:, i, width:].astype(F32) - bias_ref[:, i * part : (i + 1) * part])
        fresh = jnp.sum(fresh, axis=1, keepdims=True)
        out_ref[:count, :] = pre
        out_ref[count : count + 1, :] = spread(jnp.sum(dec_sq, axis=1, keepdims=True))
        out_ref[count + 1 : count + 2, :] = spread(jnp.sum(enc_sq, axis=1, keepdims=True))
        for i in range(extra):
            out_ref[count + 2 + i : count + 3 + i, :] = spread(fresh[i * lanes : (i + 1) * lanes])
        out_ref[count + 2 + extra :, :] = squares_ref[...]

    return pl.pallas_call(
        body,
        out_shape=pinned((count + 2 + extra + tok_dev, lat_dev), F32),
        in_specs=[pl.BlockSpec(memory_space=pltpu.VMEM)] * 5,
        out_specs=pl.BlockSpec(memory_space=pltpu.VMEM),
        name="compared",
    )(*in_vmem(got, b_dec, squares, w_enc, w_dec))


def encoded(own, peer, b_enc, mask, living, w_enc, w_dec, owners):
    count, lat_dev = mask.shape
    width = w_dec.shape[1]
    tok_dev = count // owners
    pieces = 4
    chunk = width // pieces

    def body(own_ref, peer_ref, bias_ref, mask_ref, living_ref, _, dec_ref, out_ref):
        total = own_ref[: count + 2, :] + peer_ref[: count + 2, :]
        codes = (jnp.maximum(total[:count] + bias_ref[...], 0.0) * mask_ref[...]).astype(BF16)
        for i in range(pieces):
            columns = slice(i * chunk, (i + 1) * chunk)
            part = jnp.dot(codes, dec_ref[:, columns], preferred_element_type=F32).astype(BF16)
            out_ref[:, :, columns] = part.reshape(owners, tok_dev, chunk)
        norms = jnp.sqrt(total[count : count + 2])
        alive = jnp.broadcast_to(norms[1:2] * living_ref[...], (count, lat_dev))
        side = jnp.concatenate([codes.astype(F32) * norms[0:1], alive], axis=1)
        high = side.astype(BF16)
        low = (side - high.astype(F32)).astype(BF16)
        out_ref[:, :, width:] = jnp.concatenate([high, low], axis=1).reshape(owners, tok_dev, 4 * lat_dev)

    shape = (owners, tok_dev, width + 4 * lat_dev)
    return pl.pallas_call(
        body,
        out_shape=(pltpu.VMEM if small(shape, BF16) else jax.ShapeDtypeStruct)(shape, BF16),
        in_specs=[pl.BlockSpec(memory_space=pltpu.VMEM)] * 7,
        out_specs=pl.BlockSpec(memory_space=pltpu.VMEM),
        name="encoded",
    )(*in_vmem(own, peer, b_enc, mask, living, w_enc, w_dec))


def finished(summed, got, b_dec, total, place, w_enc, w_dec, living):
    owners, tok_dev, _ = got.shape
    lat_dev, width = w_dec.shape
    part = width // tok_dev
    pieces = 2
    chunk = part // pieces
    steps = tok_dev * pieces

    def column(row, size):
        rows, lanes = (lax.broadcasted_iota(jnp.int32, (size, row.shape[1]), i) for i in range(2))
        return jnp.sum(jnp.where(rows == lanes, row, 0.0), axis=1, keepdims=True)

    def body(summed_ref, got_ref, bias_ref, total_ref, place_ref, enc_ref, dec_ref, new_enc_ref, new_dec_ref,
             enc_buffer, dec_buffer, sems):
        first = width + lat_dev
        norms = summed_ref[0:1, first : first + lat_dev] + summed_ref[0:1, first + 2 * lat_dev : first + 3 * lat_dev]
        level = 0.2 * (jnp.sum(norms, axis=1, keepdims=True) / living)
        lanes = min(owners, lat_dev)
        fresh_sq = jnp.concatenate(
            [column(total_ref[2 + i : 3 + i, :], lanes) for i in range(owners // lanes)], axis=0)
        scale = lax.rsqrt(fresh_sq + EPS)
        again = lax.rsqrt(fresh_sq / (fresh_sq + EPS) + EPS)
        alive = lax.rsqrt(column(total_ref[0:1, :], lat_dev) + EPS)
        dead = jnp.sum(place_ref[...].astype(F32), axis=1, keepdims=True) > 0.0
        copies = []

        def send(buffer, out_ref, columns):
            copy = pltpu.make_async_copy(buffer.at[:, columns], out_ref.at[:, columns], sems.at[len(copies)])
            copy.start()
            copies.append(copy)

        for i in range(steps):
            columns = slice(i * chunk, (i + 1) * chunk)
            lane = width + i % pieces * chunk
            unit = (got_ref[:, i // pieces, lane : lane + chunk].astype(F32) - bias_ref[:, columns]) * scale
            placed = jnp.dot(place_ref[...], (level * unit).astype(BF16), preferred_element_type=F32)
            enc_buffer[:, columns] = jnp.where(dead, placed, enc_ref[:, columns].astype(F32)).astype(BF16)
            send(enc_buffer, new_enc_ref, columns)
            placed = jnp.dot(place_ref[...], (unit * again).astype(BF16), preferred_element_type=F32)
            dec_buffer[:, columns] = jnp.where(dead, placed, dec_ref[:, columns].astype(F32) * alive).astype(BF16)
            send(dec_buffer, new_dec_ref, columns)
        for copy in copies:
            copy.wait()

    like = jax.ShapeDtypeStruct(w_dec.shape, BF16)
    return pl.pallas_call(
        body,
        out_shape=(like, like),
        in_specs=[pl.BlockSpec(memory_space=pltpu.VMEM)] * 7,
        out_specs=[pl.BlockSpec(memory_space=pl.ANY)] * 2,
        scratch_shapes=[pltpu.VMEM(w_dec.shape, BF16)] * 2 + [pltpu.SemaphoreType.DMA((2 * steps,))],
        name="finished",
    )(*in_vmem(summed, got, b_dec, total, place, w_enc, w_dec))


def lost(error, peer_error, total, summed, latents):
    tok_dev, lat_dev = error.shape
    width = summed.shape[1] - 4 * lat_dev
    full = width * lax.axis_size("hidden")

    def body(error_ref, peer_ref, total_ref, summed_ref, out_ref):
        mean_error = jnp.sum(error_ref[...] + peer_ref[...], axis=1, keepdims=True) / full
        mean_input = jnp.sum(total_ref[total_ref.shape[0] - tok_dev :, :], axis=1, keepdims=True) / full
        terms = summed_ref[:, width : width + lat_dev] + summed_ref[:, width + 2 * lat_dev : width + 3 * lat_dev]
        penalty = jnp.sum(terms, axis=1, keepdims=True)
        column = mean_error / (mean_input + EPS) + 5.0 * penalty / latents
        down, along = (lax.broadcasted_iota(jnp.int32, (tok_dev, tok_dev), i) for i in range(2))
        out_ref[...] = jnp.sum(jnp.where(down == along, column, 0.0), axis=0, keepdims=True)

    return pl.pallas_call(
        body,
        out_shape=jax.ShapeDtypeStruct((1, tok_dev), F32),
        in_specs=[pl.BlockSpec(memory_space=pltpu.VMEM)] * 4,
        out_specs=pl.BlockSpec(memory_space=pltpu.VMEM),
        name="lost",
    )(*in_vmem(error, peer_error, total, summed))[0]


def local(tokens, b_dec, w_enc, b_enc, w_dec, bias_moments, pool, active_blocks, dead_ids, row_ids):
    lat_dev, width = w_enc.shape
    owners = lax.axis_size("latent")
    tok_dev = tokens.shape[0]
    latents, count = lat_dev * owners, tok_dev * owners
    dead = dead_ids.shape[0]
    order = middle_out(owners)
    members = jnp.array(order, jnp.int32)[:, None]

    sent, mask, place, living, centered, squares, b_dec, b_enc, w_enc, w_dec, new_b_enc, new_moments = prepared(
        tokens, pool, dead_ids[None], row_ids[None], members, active_blocks, b_enc[None], bias_moments, b_dec[None],
        w_enc, w_dec)
    got = lax.all_to_all(sent, "latent", 0, 0, axis_index_groups=[order])
    message = compared(got, b_dec, squares, w_enc, w_dec)
    peer = swap(message)
    sent = encoded(message, peer, b_enc, mask, living, w_enc, w_dec, owners)
    summed = lax.all_to_all(sent, "latent", 0, 0, axis_index_groups=[order])
    summed, got, message, peer = lax.optimization_barrier((summed, got, message, peer))
    total = message[count:] + peer[count:]
    summed = jnp.sum(summed.astype(F32), axis=0)
    residual = centered - summed[:, :width]
    error_part = jnp.sum(jnp.square(residual).reshape(tok_dev, -1, 128), axis=1)
    error_peer = swap(error_part)
    new_enc, new_dec = finished(summed, got, b_dec, total, place, w_enc, w_dec, latents - dead)
    error_peer, new_enc, new_dec = lax.optimization_barrier((error_peer, new_enc, new_dec))
    losses = lost(error_part, error_peer, total, summed, latents)
    return losses, new_enc, new_dec, new_b_enc[0], new_moments


def solution(mesh):
    both = P(("groups", "latent"), "hidden")
    one = P(("groups", "latent"))
    return jax.shard_map(
        local,
        mesh=mesh,
        in_specs=(both, P(("groups", "hidden")), both, one, both, P(None, ("groups", "latent")), both,
                  P("groups", None), P("groups"), P("groups")),
        out_specs=(one, both, both, one, P(None, ("groups", "latent"))),
        check_vma=False,
    )
```

```python
import math

import jax
import jax.numpy as jnp
from jax import lax
from jax.experimental import pallas as pl
from jax.experimental.pallas import tpu as pltpu
from jax.sharding import PartitionSpec as P

BLOCK = 32
EPS = 1e-06
F32, BF16 = jnp.float32, jnp.bfloat16


def swap(x):
    return lax.ppermute(x, "hidden", [(0, 1), (1, 0)])


def member_order(owners):
    if owners == 8:
        return [5, 2, 6, 4, 1, 0, 7, 3]
    return sorted(range(owners), key=lambda i: (abs(4 * (i // 2) - owners + 2), i // 2, abs(2 * i - owners + 1)))


def small(shape, dtype):
    return math.prod(shape) * jnp.dtype(dtype).itemsize <= 1 << 20


def in_vmem(*arrays):
    return [pltpu.with_memory_space_constraint(x, pltpu.VMEM) if small(x.shape, x.dtype) else x for x in arrays]


def pinned(shape, dtype):
    return (pltpu.VMEM if small(shape, dtype) else jax.ShapeDtypeStruct)(shape, dtype)


def prepared(tokens, pool, dead_ids, row_ids, order, active_blocks, b_enc, moments, b_dec, w_enc, w_dec):
    tok_dev, width = tokens.shape
    lat_dev = w_enc.shape[0]
    pool_dev, owners = pool.shape[0], order.shape[0]
    dead, tiles = dead_ids.shape[1], active_blocks.shape[0]
    part = width // tok_dev
    members = member_order(owners)

    def body(*refs):
        sources, (tokens_ref, pool_ref, dead_ref, row_ref, order_ref, active_ref, moments_ref) = refs[:11], refs[23:30]
        out_ref, mask_ref, place_ref, living_ref, centered_ref, squares_ref = refs[11:17]
        bias_ref, enc_bias_ref, enc_ref, dec_ref, new_bias_ref, new_moments_ref = refs[17:23]
        bias_buffer, moments_buffer, sems = refs[30:]
        targets = (tokens_ref, pool_ref, dead_ref, row_ref, order_ref, active_ref, moments_ref,
                   bias_ref, enc_bias_ref, enc_ref, dec_ref)
        copies = [pltpu.make_async_copy(x, y, sems.at[i]) for i, (x, y) in enumerate(zip(sources, targets))]
        for copy in copies:
            copy.start()
        for copy in copies[:9]:
            copy.wait()
        me = lax.axis_index("latent")
        first = order_ref[...] * lat_dev
        there = (dead_ref[...] >= first) & (dead_ref[...] < first + lat_dev)
        slot = lax.broadcasted_iota(jnp.int32, (pool_dev, dead), 0) + me * pool_dev
        goes = jnp.where(there, 1.0, 0.0).astype(BF16)
        lies = jnp.where(row_ref[...] == slot, 1.0, 0.0).astype(BF16)
        take = lax.dot_general(goes, lies, (((1,), (1,)), ((), ())), preferred_element_type=F32).astype(BF16)
        rows = jnp.dot(take, pool_ref[...], preferred_element_type=F32)
        for dest in range(owners):
            out_ref[dest, :, :width] = tokens_ref[...]
        for piece in range(tok_dev):
            out_ref[:, piece, width:] = rows[:, piece * part : (piece + 1) * part].astype(BF16)

        ids = lax.broadcasted_iota(jnp.int32, (lat_dev, dead), 0) + me * lat_dev
        hit = jnp.where(dead_ref[...] == ids, 1.0, 0.0).astype(BF16)
        held = order_ref[...] * pool_dev
        source = jnp.where((row_ref[...] >= held) & (row_ref[...] < held + pool_dev), 1.0, 0.0).astype(BF16)
        across = (((1,), (1,)), ((), ()))
        place_ref[...] = lax.dot_general(hit, source, across, preferred_element_type=F32).astype(BF16)
        hits = lax.dot_general(jnp.ones((8, dead), BF16), hit, across, preferred_element_type=F32)
        living = jnp.where(hits[0:1] > 0.0, 0.0, 1.0)
        living_ref[...] = living
        bias_buffer[...] = enc_bias_ref[...] * living
        moments_buffer[...] = moments_ref[...] * living
        results = [pltpu.make_async_copy(bias_buffer, new_bias_ref, sems.at[11]),
                   pltpu.make_async_copy(moments_buffer, new_moments_ref, sems.at[12])]
        for copy in results:
            copy.start()
        block = lax.broadcasted_iota(jnp.int32, (tiles, lat_dev), 1) // BLOCK
        listed = jnp.zeros((tiles, lat_dev), F32)
        for i in range(lat_dev // BLOCK):
            here = jnp.where(active_ref[...] == me * (lat_dev // BLOCK) + i, 1.0, 0.0)
            listed = jnp.where(block == i, jnp.max(here, axis=1, keepdims=True), listed)
        for i, member in enumerate(members):
            tile = member * tiles // owners
            mask_ref[i * tok_dev : (i + 1) * tok_dev, :] = jnp.broadcast_to(listed[tile : tile + 1], (tok_dev, lat_dev))
        centered = tokens_ref[...].astype(F32) - bias_ref[...]
        centered_ref[...] = centered
        squares = jnp.zeros((tok_dev, lat_dev), F32)
        for i in range(width // lat_dev):
            lanes = centered[:, i * lat_dev : (i + 1) * lat_dev]
            squares = squares + lanes * lanes
        squares_ref[...] = squares
        for copy in copies[9:] + results:
            copy.wait()

    given = (tokens, pool, dead_ids, row_ids, order, active_blocks, moments, b_dec, b_enc, w_enc, w_dec)
    on_device, small_results = pl.BlockSpec(memory_space=pltpu.VMEM), (b_enc, moments)
    return pl.pallas_call(
        body,
        out_shape=(
            pinned((owners, tok_dev, width + part), BF16),
            pinned((owners * tok_dev, lat_dev), F32),
            pinned((lat_dev, owners), BF16),
            pinned((1, lat_dev), F32),
            pinned((tok_dev, width), F32),
            pinned((tok_dev, lat_dev), F32),
            *(pinned(x.shape, x.dtype) for x in given[7:]),
            *(jax.ShapeDtypeStruct(x.shape, x.dtype) for x in small_results),
        ),
        in_specs=[pl.BlockSpec(memory_space=pl.ANY)] * 11,
        out_specs=[on_device] * 10 + [pl.BlockSpec(memory_space=pl.ANY)] * 2,
        scratch_shapes=[pltpu.VMEM(x.shape, x.dtype) for x in given[:7] + small_results]
        + [pltpu.SemaphoreType.DMA((13,))],
        name="prepared",
    )(*given)


def compared(got, b_dec, squares, w_enc, w_dec):
    owners, tok_dev, _ = got.shape
    lat_dev, width = w_enc.shape
    count, part = owners * tok_dev, width // tok_dev
    pieces = 4
    chunk = width // pieces
    lanes = min(owners, lat_dev)
    extra = owners // lanes

    def spread(column):
        size = column.shape[0]
        down, along = (lax.broadcasted_iota(jnp.int32, (size, lat_dev), i) for i in range(2))
        return jnp.sum(jnp.where(down == along, column, 0.0), axis=0, keepdims=True)

    def folded(x):
        total = x[:, :lat_dev] * x[:, :lat_dev]
        for i in range(1, x.shape[1] // lat_dev):
            piece = x[:, i * lat_dev : (i + 1) * lat_dev]
            total = total + piece * piece
        return total

    def body(got_ref, bias_ref, squares_ref, enc_ref, dec_ref, out_ref):
        pre = jnp.zeros((count, lat_dev), F32)
        enc_sq = jnp.zeros((lat_dev, lat_dev), F32)
        dec_sq = jnp.zeros((lat_dev, lat_dev), F32)
        for i in range(pieces):
            columns = slice(i * chunk, (i + 1) * chunk)
            rows = got_ref[:, :, columns].reshape(count, chunk).astype(F32)
            centered = (rows - bias_ref[:, columns]).astype(BF16)
            pre = pre + lax.dot_general(
                centered, enc_ref[:, columns], (((1,), (1,)), ((), ())), preferred_element_type=F32)
            enc_sq = enc_sq + folded(enc_ref[:, columns].astype(F32))
            dec_sq = dec_sq + folded(dec_ref[:, columns].astype(F32))
        fresh = jnp.zeros((owners, lat_dev), F32)
        for i in range(tok_dev):
            fresh = fresh + folded(got_ref[:, i, width:].astype(F32) - bias_ref[:, i * part : (i + 1) * part])
        fresh = jnp.sum(fresh, axis=1, keepdims=True)
        out_ref[:count, :] = pre
        out_ref[count : count + 1, :] = spread(jnp.sum(dec_sq, axis=1, keepdims=True))
        out_ref[count + 1 : count + 2, :] = spread(jnp.sum(enc_sq, axis=1, keepdims=True))
        for i in range(extra):
            out_ref[count + 2 + i : count + 3 + i, :] = spread(fresh[i * lanes : (i + 1) * lanes])
        out_ref[count + 2 + extra :, :] = squares_ref[...]

    return pl.pallas_call(
        body,
        out_shape=pinned((count + 2 + extra + tok_dev, lat_dev), F32),
        in_specs=[pl.BlockSpec(memory_space=pltpu.VMEM)] * 5,
        out_specs=pl.BlockSpec(memory_space=pltpu.VMEM),
        name="compared",
    )(*in_vmem(got, b_dec, squares, w_enc, w_dec))


def encoded(own, peer, b_enc, mask, living, w_enc, w_dec, owners):
    count, lat_dev = mask.shape
    width = w_dec.shape[1]
    tok_dev = count // owners
    pieces = 4
    chunk = width // pieces

    def body(own_ref, peer_ref, bias_ref, mask_ref, living_ref, _, dec_ref, out_ref):
        total = own_ref[: count + 2, :] + peer_ref[: count + 2, :]
        codes = (jnp.maximum(total[:count] + bias_ref[...], 0.0) * mask_ref[...]).astype(BF16)
        for i in range(pieces):
            columns = slice(i * chunk, (i + 1) * chunk)
            part = jnp.dot(codes, dec_ref[:, columns], preferred_element_type=F32).astype(BF16)
            out_ref[:, :, columns] = part.reshape(owners, tok_dev, chunk)
        norms = jnp.sqrt(total[count : count + 2])
        alive = jnp.broadcast_to(norms[1:2] * living_ref[...], (count, lat_dev))
        side = jnp.concatenate([codes.astype(F32) * norms[0:1], alive], axis=1)
        high = side.astype(BF16)
        low = (side - high.astype(F32)).astype(BF16)
        out_ref[:, :, width:] = jnp.concatenate([high, low], axis=1).reshape(owners, tok_dev, 4 * lat_dev)

    shape = (owners, tok_dev, width + 4 * lat_dev)
    return pl.pallas_call(
        body,
        out_shape=(pltpu.VMEM if small(shape, BF16) else jax.ShapeDtypeStruct)(shape, BF16),
        in_specs=[pl.BlockSpec(memory_space=pltpu.VMEM)] * 7,
        out_specs=pl.BlockSpec(memory_space=pltpu.VMEM),
        name="encoded",
    )(*in_vmem(own, peer, b_enc, mask, living, w_enc, w_dec))


def finished(summed, got, b_dec, total, place, w_enc, w_dec, living):
    owners, tok_dev, _ = got.shape
    lat_dev, width = w_dec.shape
    part = width // tok_dev
    pieces = 2
    chunk = part // pieces
    steps = tok_dev * pieces

    def column(row, size):
        rows, lanes = (lax.broadcasted_iota(jnp.int32, (size, row.shape[1]), i) for i in range(2))
        return jnp.sum(jnp.where(rows == lanes, row, 0.0), axis=1, keepdims=True)

    def body(summed_ref, got_ref, bias_ref, total_ref, place_ref, enc_ref, dec_ref, new_enc_ref, new_dec_ref,
             enc_buffer, dec_buffer, sems):
        first = width + lat_dev
        norms = summed_ref[0:1, first : first + lat_dev] + summed_ref[0:1, first + 2 * lat_dev : first + 3 * lat_dev]
        level = 0.2 * (jnp.sum(norms, axis=1, keepdims=True) / living)
        lanes = min(owners, lat_dev)
        fresh_sq = jnp.concatenate(
            [column(total_ref[2 + i : 3 + i, :], lanes) for i in range(owners // lanes)], axis=0)
        scale = lax.rsqrt(fresh_sq + EPS)
        again = lax.rsqrt(fresh_sq / (fresh_sq + EPS) + EPS)
        alive = lax.rsqrt(column(total_ref[0:1, :], lat_dev) + EPS)
        dead = jnp.sum(place_ref[...].astype(F32), axis=1, keepdims=True) > 0.0
        copies = []

        def send(buffer, out_ref, columns):
            copy = pltpu.make_async_copy(buffer.at[:, columns], out_ref.at[:, columns], sems.at[len(copies)])
            copy.start()
            copies.append(copy)

        for i in range(steps):
            columns = slice(i * chunk, (i + 1) * chunk)
            lane = width + i % pieces * chunk
            unit = (got_ref[:, i // pieces, lane : lane + chunk].astype(F32) - bias_ref[:, columns]) * scale
            placed = jnp.dot(place_ref[...], (level * unit).astype(BF16), preferred_element_type=F32)
            enc_buffer[:, columns] = jnp.where(dead, placed, enc_ref[:, columns].astype(F32)).astype(BF16)
            send(enc_buffer, new_enc_ref, columns)
            placed = jnp.dot(place_ref[...], (unit * again).astype(BF16), preferred_element_type=F32)
            dec_buffer[:, columns] = jnp.where(dead, placed, dec_ref[:, columns].astype(F32) * alive).astype(BF16)
            send(dec_buffer, new_dec_ref, columns)
        for copy in copies:
            copy.wait()

    like = jax.ShapeDtypeStruct(w_dec.shape, BF16)
    return pl.pallas_call(
        body,
        out_shape=(like, like),
        in_specs=[pl.BlockSpec(memory_space=pltpu.VMEM)] * 7,
        out_specs=[pl.BlockSpec(memory_space=pl.ANY)] * 2,
        scratch_shapes=[pltpu.VMEM(w_dec.shape, BF16)] * 2 + [pltpu.SemaphoreType.DMA((2 * steps,))],
        name="finished",
    )(*in_vmem(summed, got, b_dec, total, place, w_enc, w_dec))


def lost(error, peer_error, total, summed, latents):
    tok_dev, lat_dev = error.shape
    width = summed.shape[1] - 4 * lat_dev
    full = width * lax.axis_size("hidden")

    def body(error_ref, peer_ref, total_ref, summed_ref, out_ref):
        mean_error = jnp.sum(error_ref[...] + peer_ref[...], axis=1, keepdims=True) / full
        mean_input = jnp.sum(total_ref[total_ref.shape[0] - tok_dev :, :], axis=1, keepdims=True) / full
        terms = summed_ref[:, width : width + lat_dev] + summed_ref[:, width + 2 * lat_dev : width + 3 * lat_dev]
        penalty = jnp.sum(terms, axis=1, keepdims=True)
        column = mean_error / (mean_input + EPS) + 5.0 * penalty / latents
        down, along = (lax.broadcasted_iota(jnp.int32, (tok_dev, tok_dev), i) for i in range(2))
        out_ref[...] = jnp.sum(jnp.where(down == along, column, 0.0), axis=0, keepdims=True)

    return pl.pallas_call(
        body,
        out_shape=jax.ShapeDtypeStruct((1, tok_dev), F32),
        in_specs=[pl.BlockSpec(memory_space=pltpu.VMEM)] * 4,
        out_specs=pl.BlockSpec(memory_space=pltpu.VMEM),
        name="lost",
    )(*in_vmem(error, peer_error, total, summed))[0]


def local(tokens, b_dec, w_enc, b_enc, w_dec, bias_moments, pool, active_blocks, dead_ids, row_ids):
    lat_dev, width = w_enc.shape
    owners = lax.axis_size("latent")
    tok_dev = tokens.shape[0]
    latents, count = lat_dev * owners, tok_dev * owners
    dead = dead_ids.shape[0]
    order = member_order(owners)
    members = jnp.array(order, jnp.int32)[:, None]

    sent, mask, place, living, centered, squares, b_dec, b_enc, w_enc, w_dec, new_b_enc, new_moments = prepared(
        tokens, pool, dead_ids[None], row_ids[None], members, active_blocks, b_enc[None], bias_moments, b_dec[None],
        w_enc, w_dec)
    got = lax.all_to_all(sent, "latent", 0, 0, axis_index_groups=[order])
    message = compared(got, b_dec, squares, w_enc, w_dec)
    peer = swap(message)
    sent = encoded(message, peer, b_enc, mask, living, w_enc, w_dec, owners)
    summed = lax.all_to_all(sent, "latent", 0, 0, axis_index_groups=[order])
    summed, got, message, peer = lax.optimization_barrier((summed, got, message, peer))
    total = message[count:] + peer[count:]
    summed = jnp.sum(summed.astype(F32), axis=0)
    residual = centered - summed[:, :width]
    error_part = jnp.sum(jnp.square(residual).reshape(tok_dev, -1, 128), axis=1)
    error_peer = swap(error_part)
    new_enc, new_dec = finished(summed, got, b_dec, total, place, w_enc, w_dec, latents - dead)
    error_peer, new_enc, new_dec = lax.optimization_barrier((error_peer, new_enc, new_dec))
    losses = lost(error_part, error_peer, total, summed, latents)
    return losses, new_enc, new_dec, new_b_enc[0], new_moments


def solution(mesh):
    both = P(("groups", "latent"), "hidden")
    one = P(("groups", "latent"))
    return jax.shard_map(
        local,
        mesh=mesh,
        in_specs=(both, P(("groups", "hidden")), both, one, both, P(None, ("groups", "latent")), both,
                  P("groups", None), P("groups"), P("groups")),
        out_specs=(one, both, both, one, P(None, ("groups", "latent"))),
        check_vma=False,
    )
```

```python
import math

import jax
import jax.numpy as jnp
from jax import lax
from jax.experimental import pallas as pl
from jax.experimental.pallas import tpu as pltpu
from jax.sharding import PartitionSpec as P

BLOCK = 32
EPS = 1e-06
F32, BF16 = jnp.float32, jnp.bfloat16


def swap(x):
    return lax.ppermute(x, "hidden", [(0, 1), (1, 0)])


def member_order(owners):
    if owners == 8:
        return [5, 2, 6, 4, 1, 0, 7, 3]
    return sorted(range(owners), key=lambda i: (abs(4 * (i // 2) - owners + 2), i // 2, abs(2 * i - owners + 1)))


def small(shape, dtype):
    return math.prod(shape) * jnp.dtype(dtype).itemsize <= 1 << 20


def in_vmem(*arrays):
    return [pltpu.with_memory_space_constraint(x, pltpu.VMEM) if small(x.shape, x.dtype) else x for x in arrays]


def pinned(shape, dtype):
    return (pltpu.VMEM if small(shape, dtype) else jax.ShapeDtypeStruct)(shape, dtype)


def prepared(tokens, pool, dead_ids, row_ids, order, active_blocks, b_enc, b_dec, w_enc, w_dec):
    tok_dev, width = tokens.shape
    lat_dev = w_enc.shape[0]
    pool_dev, owners = pool.shape[0], order.shape[0]
    dead, tiles = dead_ids.shape[1], active_blocks.shape[0]
    part = width // tok_dev
    members = member_order(owners)

    def body(*refs):
        sources, (tokens_ref, pool_ref, dead_ref, row_ref, order_ref, active_ref) = refs[:10], refs[20:26]
        out_ref, mask_ref, place_ref, living_ref, centered_ref, squares_ref = refs[10:16]
        bias_ref, enc_bias_ref, enc_ref, dec_ref = refs[16:20]
        sems = refs[26]
        targets = (tokens_ref, pool_ref, dead_ref, row_ref, order_ref, active_ref,
                   bias_ref, enc_bias_ref, enc_ref, dec_ref)
        copies = [pltpu.make_async_copy(x, y, sems.at[i]) for i, (x, y) in enumerate(zip(sources, targets))]
        for copy in copies:
            copy.start()
        for copy in copies[:7]:
            copy.wait()
        me = lax.axis_index("latent")
        first = order_ref[...] * lat_dev
        there = (dead_ref[...] >= first) & (dead_ref[...] < first + lat_dev)
        slot = lax.broadcasted_iota(jnp.int32, (pool_dev, dead), 0) + me * pool_dev
        goes = jnp.where(there, 1.0, 0.0).astype(BF16)
        lies = jnp.where(row_ref[...] == slot, 1.0, 0.0).astype(BF16)
        take = lax.dot_general(goes, lies, (((1,), (1,)), ((), ())), preferred_element_type=F32).astype(BF16)
        rows = jnp.dot(take, pool_ref[...], preferred_element_type=F32)
        for dest in range(owners):
            out_ref[dest, :, :width] = tokens_ref[...]
        for piece in range(tok_dev):
            out_ref[:, piece, width:] = rows[:, piece * part : (piece + 1) * part].astype(BF16)

        ids = lax.broadcasted_iota(jnp.int32, (lat_dev, dead), 0) + me * lat_dev
        hit = jnp.where(dead_ref[...] == ids, 1.0, 0.0).astype(BF16)
        held = order_ref[...] * pool_dev
        source = jnp.where((row_ref[...] >= held) & (row_ref[...] < held + pool_dev), 1.0, 0.0).astype(BF16)
        across = (((1,), (1,)), ((), ()))
        place_ref[...] = lax.dot_general(hit, source, across, preferred_element_type=F32).astype(BF16)
        hits = lax.dot_general(jnp.ones((8, dead), BF16), hit, across, preferred_element_type=F32)
        living_ref[...] = jnp.where(hits[0:1] > 0.0, 0.0, 1.0)
        block = lax.broadcasted_iota(jnp.int32, (tiles, lat_dev), 1) // BLOCK
        listed = jnp.zeros((tiles, lat_dev), F32)
        for i in range(lat_dev // BLOCK):
            here = jnp.where(active_ref[...] == me * (lat_dev // BLOCK) + i, 1.0, 0.0)
            listed = jnp.where(block == i, jnp.max(here, axis=1, keepdims=True), listed)
        for i, member in enumerate(members):
            tile = member * tiles // owners
            mask_ref[i * tok_dev : (i + 1) * tok_dev, :] = jnp.broadcast_to(listed[tile : tile + 1], (tok_dev, lat_dev))
        centered = tokens_ref[...].astype(F32) - bias_ref[...]
        centered_ref[...] = centered
        squares = jnp.zeros((tok_dev, lat_dev), F32)
        for i in range(width // lat_dev):
            lanes = centered[:, i * lat_dev : (i + 1) * lat_dev]
            squares = squares + lanes * lanes
        squares_ref[...] = squares
        for copy in copies[7:]:
            copy.wait()

    given = (tokens, pool, dead_ids, row_ids, order, active_blocks, b_dec, b_enc, w_enc, w_dec)
    return pl.pallas_call(
        body,
        out_shape=(
            pinned((owners, tok_dev, width + part), BF16),
            pinned((owners * tok_dev, lat_dev), F32),
            pinned((lat_dev, owners), BF16),
            pinned((1, lat_dev), F32),
            pinned((tok_dev, width), F32),
            pinned((tok_dev, lat_dev), F32),
            *(pinned(x.shape, x.dtype) for x in given[6:]),
        ),
        in_specs=[pl.BlockSpec(memory_space=pl.ANY)] * 10,
        out_specs=[pl.BlockSpec(memory_space=pltpu.VMEM)] * 10,
        scratch_shapes=[pltpu.VMEM(x.shape, x.dtype) for x in given[:6]] + [pltpu.SemaphoreType.DMA((10,))],
        name="prepared",
    )(*given)


def compared(got, b_dec, squares, w_enc, w_dec):
    owners, tok_dev, _ = got.shape
    lat_dev, width = w_enc.shape
    count, part = owners * tok_dev, width // tok_dev
    pieces = 4
    chunk = width // pieces
    lanes = min(owners, lat_dev)
    extra = owners // lanes

    def spread(column):
        size = column.shape[0]
        down, along = (lax.broadcasted_iota(jnp.int32, (size, lat_dev), i) for i in range(2))
        return jnp.sum(jnp.where(down == along, column, 0.0), axis=0, keepdims=True)

    def folded(x):
        total = x[:, :lat_dev] * x[:, :lat_dev]
        for i in range(1, x.shape[1] // lat_dev):
            piece = x[:, i * lat_dev : (i + 1) * lat_dev]
            total = total + piece * piece
        return total

    def body(got_ref, bias_ref, squares_ref, enc_ref, dec_ref, out_ref):
        pre = jnp.zeros((count, lat_dev), F32)
        enc_sq = jnp.zeros((lat_dev, lat_dev), F32)
        dec_sq = jnp.zeros((lat_dev, lat_dev), F32)
        for i in range(pieces):
            columns = slice(i * chunk, (i + 1) * chunk)
            rows = got_ref[:, :, columns].reshape(count, chunk).astype(F32)
            centered = (rows - bias_ref[:, columns]).astype(BF16)
            pre = pre + lax.dot_general(
                centered, enc_ref[:, columns], (((1,), (1,)), ((), ())), preferred_element_type=F32)
            enc_sq = enc_sq + folded(enc_ref[:, columns].astype(F32))
            dec_sq = dec_sq + folded(dec_ref[:, columns].astype(F32))
        fresh = jnp.zeros((owners, lat_dev), F32)
        for i in range(tok_dev):
            fresh = fresh + folded(got_ref[:, i, width:].astype(F32) - bias_ref[:, i * part : (i + 1) * part])
        fresh = jnp.sum(fresh, axis=1, keepdims=True)
        out_ref[:count, :] = pre
        out_ref[count : count + 1, :] = spread(jnp.sum(dec_sq, axis=1, keepdims=True))
        out_ref[count + 1 : count + 2, :] = spread(jnp.sum(enc_sq, axis=1, keepdims=True))
        for i in range(extra):
            out_ref[count + 2 + i : count + 3 + i, :] = spread(fresh[i * lanes : (i + 1) * lanes])
        out_ref[count + 2 + extra :, :] = squares_ref[...]

    return pl.pallas_call(
        body,
        out_shape=pinned((count + 2 + extra + tok_dev, lat_dev), F32),
        in_specs=[pl.BlockSpec(memory_space=pltpu.VMEM)] * 5,
        out_specs=pl.BlockSpec(memory_space=pltpu.VMEM),
        name="compared",
    )(*in_vmem(got, b_dec, squares, w_enc, w_dec))


def encoded(own, peer, b_enc, mask, living, w_enc, w_dec, owners):
    count, lat_dev = mask.shape
    width = w_dec.shape[1]
    tok_dev = count // owners
    pieces = 4
    chunk = width // pieces

    def body(own_ref, peer_ref, bias_ref, mask_ref, living_ref, _, dec_ref, out_ref):
        total = own_ref[: count + 2, :] + peer_ref[: count + 2, :]
        codes = (jnp.maximum(total[:count] + bias_ref[...], 0.0) * mask_ref[...]).astype(BF16)
        for i in range(pieces):
            columns = slice(i * chunk, (i + 1) * chunk)
            part = jnp.dot(codes, dec_ref[:, columns], preferred_element_type=F32).astype(BF16)
            out_ref[:, :, columns] = part.reshape(owners, tok_dev, chunk)
        norms = jnp.sqrt(total[count : count + 2])
        alive = jnp.broadcast_to(norms[1:2] * living_ref[...], (count, lat_dev))
        side = jnp.concatenate([codes.astype(F32) * norms[0:1], alive], axis=1)
        high = side.astype(BF16)
        low = (side - high.astype(F32)).astype(BF16)
        out_ref[:, :, width:] = jnp.concatenate([high, low], axis=1).reshape(owners, tok_dev, 4 * lat_dev)

    shape = (owners, tok_dev, width + 4 * lat_dev)
    return pl.pallas_call(
        body,
        out_shape=(pltpu.VMEM if small(shape, BF16) else jax.ShapeDtypeStruct)(shape, BF16),
        in_specs=[pl.BlockSpec(memory_space=pltpu.VMEM)] * 7,
        out_specs=pl.BlockSpec(memory_space=pltpu.VMEM),
        name="encoded",
    )(*in_vmem(own, peer, b_enc, mask, living, w_enc, w_dec))


def finished(summed, got, b_dec, total, place, w_enc, w_dec, living, b_enc, moments, count):
    owners, tok_dev, _ = got.shape
    lat_dev, width = w_dec.shape
    part = width // tok_dev
    pieces = 2
    chunk = part // pieces
    steps = tok_dev * pieces

    def column(row, size):
        rows, lanes = (lax.broadcasted_iota(jnp.int32, (size, row.shape[1]), i) for i in range(2))
        return jnp.sum(jnp.where(rows == lanes, row, 0.0), axis=1, keepdims=True)

    def body(summed_ref, got_ref, bias_ref, total_ref, place_ref, enc_ref, dec_ref, living_ref, enc_bias_ref,
             moments_ref, new_enc_ref, new_dec_ref, new_bias_ref, new_moments_ref,
             enc_buffer, dec_buffer, bias_buffer, moments_buffer, sems):
        fetch = pltpu.make_async_copy(moments_ref, moments_buffer, sems.at[2 * steps])
        fetch.start()
        bias_buffer[...] = enc_bias_ref[...] * living_ref[...]
        first = width + lat_dev
        norms = summed_ref[0:1, first : first + lat_dev] + summed_ref[0:1, first + 2 * lat_dev : first + 3 * lat_dev]
        level = 0.2 * (jnp.sum(norms, axis=1, keepdims=True) / count)
        lanes = min(owners, lat_dev)
        fresh_sq = jnp.concatenate(
            [column(total_ref[2 + i : 3 + i, :], lanes) for i in range(owners // lanes)], axis=0)
        scale = lax.rsqrt(fresh_sq + EPS)
        again = lax.rsqrt(fresh_sq / (fresh_sq + EPS) + EPS)
        alive = lax.rsqrt(column(total_ref[0:1, :], lat_dev) + EPS)
        dead = jnp.sum(place_ref[...].astype(F32), axis=1, keepdims=True) > 0.0
        copies = []

        def send(buffer, out_ref, columns):
            copy = pltpu.make_async_copy(buffer.at[:, columns], out_ref.at[:, columns], sems.at[len(copies)])
            copy.start()
            copies.append(copy)

        for i in range(steps):
            columns = slice(i * chunk, (i + 1) * chunk)
            lane = width + i % pieces * chunk
            unit = (got_ref[:, i // pieces, lane : lane + chunk].astype(F32) - bias_ref[:, columns]) * scale
            placed = jnp.dot(place_ref[...], (level * unit).astype(BF16), preferred_element_type=F32)
            enc_buffer[:, columns] = jnp.where(dead, placed, enc_ref[:, columns].astype(F32)).astype(BF16)
            send(enc_buffer, new_enc_ref, columns)
            placed = jnp.dot(place_ref[...], (unit * again).astype(BF16), preferred_element_type=F32)
            dec_buffer[:, columns] = jnp.where(dead, placed, dec_ref[:, columns].astype(F32) * alive).astype(BF16)
            send(dec_buffer, new_dec_ref, columns)
        fetch.wait()
        moments_buffer[...] = moments_buffer[...] * living_ref[...]
        for i, (buffer, out_ref) in enumerate(((bias_buffer, new_bias_ref), (moments_buffer, new_moments_ref))):
            copy = pltpu.make_async_copy(buffer, out_ref, sems.at[2 * steps + 1 + i])
            copy.start()
            copies.append(copy)
        for copy in copies:
            copy.wait()

    like = jax.ShapeDtypeStruct(w_dec.shape, BF16)
    return pl.pallas_call(
        body,
        out_shape=(like, like, *(jax.ShapeDtypeStruct(x.shape, F32) for x in (b_enc, moments))),
        in_specs=[pl.BlockSpec(memory_space=pltpu.VMEM)] * 9 + [pl.BlockSpec(memory_space=pl.ANY)],
        out_specs=[pl.BlockSpec(memory_space=pl.ANY)] * 4,
        scratch_shapes=[pltpu.VMEM(w_dec.shape, BF16)] * 2 + [pltpu.VMEM(x.shape, F32) for x in (b_enc, moments)]
        + [pltpu.SemaphoreType.DMA((2 * steps + 3,))],
        name="finished",
    )(*in_vmem(summed, got, b_dec, total, place, w_enc, w_dec, living, b_enc), moments)


def lost(error, peer_error, total, summed, latents):
    tok_dev, lat_dev = error.shape
    width = summed.shape[1] - 4 * lat_dev
    full = width * lax.axis_size("hidden")

    def body(error_ref, peer_ref, total_ref, summed_ref, out_ref):
        mean_error = jnp.sum(error_ref[...] + peer_ref[...], axis=1, keepdims=True) / full
        mean_input = jnp.sum(total_ref[total_ref.shape[0] - tok_dev :, :], axis=1, keepdims=True) / full
        terms = summed_ref[:, width : width + lat_dev] + summed_ref[:, width + 2 * lat_dev : width + 3 * lat_dev]
        penalty = jnp.sum(terms, axis=1, keepdims=True)
        column = mean_error / (mean_input + EPS) + 5.0 * penalty / latents
        down, along = (lax.broadcasted_iota(jnp.int32, (tok_dev, tok_dev), i) for i in range(2))
        out_ref[...] = jnp.sum(jnp.where(down == along, column, 0.0), axis=0, keepdims=True)

    return pl.pallas_call(
        body,
        out_shape=jax.ShapeDtypeStruct((1, tok_dev), F32),
        in_specs=[pl.BlockSpec(memory_space=pltpu.VMEM)] * 4,
        out_specs=pl.BlockSpec(memory_space=pltpu.VMEM),
        name="lost",
    )(*in_vmem(error, peer_error, total, summed))[0]


def local(tokens, b_dec, w_enc, b_enc, w_dec, bias_moments, pool, active_blocks, dead_ids, row_ids):
    lat_dev, width = w_enc.shape
    owners = lax.axis_size("latent")
    tok_dev = tokens.shape[0]
    latents, count = lat_dev * owners, tok_dev * owners
    dead = dead_ids.shape[0]
    order = member_order(owners)
    members = jnp.array(order, jnp.int32)[:, None]

    sent, mask, place, living, centered, squares, b_dec, b_enc, w_enc, w_dec = prepared(
        tokens, pool, dead_ids[None], row_ids[None], members, active_blocks, b_enc[None], b_dec[None], w_enc, w_dec)
    got = lax.all_to_all(sent, "latent", 0, 0, axis_index_groups=[order])
    message = compared(got, b_dec, squares, w_enc, w_dec)
    peer = swap(message)
    sent = encoded(message, peer, b_enc, mask, living, w_enc, w_dec, owners)
    summed = lax.all_to_all(sent, "latent", 0, 0, axis_index_groups=[order])
    summed, got, message, peer = lax.optimization_barrier((summed, got, message, peer))
    total = message[count:] + peer[count:]
    summed = jnp.sum(summed.astype(F32), axis=0)
    residual = centered - summed[:, :width]
    error_part = jnp.sum(jnp.square(residual).reshape(tok_dev, -1, 128), axis=1)
    error_peer = swap(error_part)
    new_enc, new_dec, new_b_enc, new_moments = finished(
        summed, got, b_dec, total, place, w_enc, w_dec, living, b_enc, bias_moments, latents - dead)
    error_peer, new_enc, new_dec = lax.optimization_barrier((error_peer, new_enc, new_dec))
    losses = lost(error_part, error_peer, total, summed, latents)
    return losses, new_enc, new_dec, new_b_enc[0], new_moments


def solution(mesh):
    both = P(("groups", "latent"), "hidden")
    one = P(("groups", "latent"))
    return jax.shard_map(
        local,
        mesh=mesh,
        in_specs=(both, P(("groups", "hidden")), both, one, both, P(None, ("groups", "latent")), both,
                  P("groups", None), P("groups"), P("groups")),
        out_specs=(one, both, both, one, P(None, ("groups", "latent"))),
        check_vma=False,
    )
```

```python
import math

import jax
import jax.numpy as jnp
from jax import lax
from jax.experimental import pallas as pl
from jax.experimental.pallas import tpu as pltpu
from jax.sharding import PartitionSpec as P

BLOCK = 32
EPS = 1e-06
F32, BF16 = jnp.float32, jnp.bfloat16


def swap(x):
    return lax.ppermute(x, "hidden", [(0, 1), (1, 0)])


def member_order(owners):
    if owners == 8:
        return [5, 2, 6, 4, 1, 0, 7, 3]
    return sorted(range(owners), key=lambda i: (abs(4 * (i // 2) - owners + 2), i // 2, abs(2 * i - owners + 1)))


def small(shape, dtype):
    return math.prod(shape) * jnp.dtype(dtype).itemsize <= 1 << 20


def in_vmem(*arrays):
    return [pltpu.with_memory_space_constraint(x, pltpu.VMEM) if small(x.shape, x.dtype) else x for x in arrays]


def pinned(shape, dtype):
    return (pltpu.VMEM if small(shape, dtype) else jax.ShapeDtypeStruct)(shape, dtype)


def spread(column, lanes):
    down, along = (lax.broadcasted_iota(jnp.int32, (column.shape[0], lanes), i) for i in range(2))
    return jnp.sum(jnp.where(down == along, column, 0.0), axis=0, keepdims=True)


def folded(x, lanes):
    total = x[:, :lanes] * x[:, :lanes]
    for i in range(1, x.shape[1] // lanes):
        piece = x[:, i * lanes : (i + 1) * lanes]
        total = total + piece * piece
    return total


def prepared(tokens, pool, dead_ids, row_ids, order, active_blocks, b_enc, b_dec, w_enc, w_dec):
    tok_dev, width = tokens.shape
    lat_dev = w_enc.shape[0]
    pool_dev, owners = pool.shape[0], order.shape[0]
    dead, tiles = dead_ids.shape[1], active_blocks.shape[0]
    part = width // tok_dev
    members = member_order(owners)

    def body(*refs):
        sources, (tokens_ref, pool_ref, dead_ref, row_ref, order_ref, active_ref) = refs[:10], refs[20:26]
        out_ref, mask_ref, place_ref, living_ref, centered_ref, squares_ref = refs[10:16]
        bias_ref, enc_bias_ref, enc_ref, dec_ref = refs[16:20]
        sems = refs[26]
        targets = (tokens_ref, pool_ref, dead_ref, row_ref, order_ref, active_ref,
                   bias_ref, enc_bias_ref, enc_ref, dec_ref)
        copies = [pltpu.make_async_copy(x, y, sems.at[i]) for i, (x, y) in enumerate(zip(sources, targets))]
        for copy in copies:
            copy.start()
        for copy in copies[:7]:
            copy.wait()
        me = lax.axis_index("latent")
        first = order_ref[...] * lat_dev
        there = (dead_ref[...] >= first) & (dead_ref[...] < first + lat_dev)
        slot = lax.broadcasted_iota(jnp.int32, (pool_dev, dead), 0) + me * pool_dev
        goes = jnp.where(there, 1.0, 0.0).astype(BF16)
        lies = jnp.where(row_ref[...] == slot, 1.0, 0.0).astype(BF16)
        take = lax.dot_general(goes, lies, (((1,), (1,)), ((), ())), preferred_element_type=F32).astype(BF16)
        rows = jnp.dot(take, pool_ref[...], preferred_element_type=F32)
        for dest in range(owners):
            out_ref[dest, :, :width] = tokens_ref[...]
        for piece in range(tok_dev):
            out_ref[:, piece, width:] = rows[:, piece * part : (piece + 1) * part].astype(BF16)

        ids = lax.broadcasted_iota(jnp.int32, (lat_dev, dead), 0) + me * lat_dev
        hit = jnp.where(dead_ref[...] == ids, 1.0, 0.0).astype(BF16)
        held = order_ref[...] * pool_dev
        source = jnp.where((row_ref[...] >= held) & (row_ref[...] < held + pool_dev), 1.0, 0.0).astype(BF16)
        across = (((1,), (1,)), ((), ()))
        place_ref[...] = lax.dot_general(hit, source, across, preferred_element_type=F32).astype(BF16)
        hits = lax.dot_general(jnp.ones((8, dead), BF16), hit, across, preferred_element_type=F32)
        living_ref[...] = jnp.where(hits[0:1] > 0.0, 0.0, 1.0)
        block = lax.broadcasted_iota(jnp.int32, (tiles, lat_dev), 1) // BLOCK
        listed = jnp.zeros((tiles, lat_dev), F32)
        for i in range(lat_dev // BLOCK):
            here = jnp.where(active_ref[...] == me * (lat_dev // BLOCK) + i, 1.0, 0.0)
            listed = jnp.where(block == i, jnp.max(here, axis=1, keepdims=True), listed)
        for i, member in enumerate(members):
            tile = member * tiles // owners
            mask_ref[i * tok_dev : (i + 1) * tok_dev, :] = jnp.broadcast_to(listed[tile : tile + 1], (tok_dev, lat_dev))
        centered = tokens_ref[...].astype(F32) - bias_ref[...]
        centered_ref[...] = centered
        squares_ref[1:, :] = folded(centered, lat_dev)
        for copy in copies[7:9]:
            copy.wait()
        enc_sq = jnp.zeros((lat_dev, lat_dev), F32)
        for i in range(4):
            enc_sq = enc_sq + folded(enc_ref[:, i * width // 4 : (i + 1) * width // 4].astype(F32), lat_dev)
        squares_ref[0:1, :] = spread(jnp.sum(enc_sq, axis=1, keepdims=True), lat_dev)
        copies[9].wait()

    given = (tokens, pool, dead_ids, row_ids, order, active_blocks, b_dec, b_enc, w_enc, w_dec)
    return pl.pallas_call(
        body,
        out_shape=(
            pinned((owners, tok_dev, width + part), BF16),
            pinned((owners * tok_dev, lat_dev), F32),
            pinned((lat_dev, owners), BF16),
            pinned((1, lat_dev), F32),
            pinned((tok_dev, width), F32),
            pinned((1 + tok_dev, lat_dev), F32),
            *(pinned(x.shape, x.dtype) for x in given[6:]),
        ),
        in_specs=[pl.BlockSpec(memory_space=pl.ANY)] * 10,
        out_specs=[pl.BlockSpec(memory_space=pltpu.VMEM)] * 10,
        scratch_shapes=[pltpu.VMEM(x.shape, x.dtype) for x in given[:6]] + [pltpu.SemaphoreType.DMA((10,))],
        name="prepared",
    )(*given)


def compared(got, b_dec, squares, w_enc, w_dec):
    owners, tok_dev, _ = got.shape
    lat_dev, width = w_enc.shape
    count, part = owners * tok_dev, width // tok_dev
    pieces = 4
    chunk = width // pieces
    lanes = min(owners, lat_dev)
    extra = owners // lanes

    def body(got_ref, bias_ref, squares_ref, enc_ref, dec_ref, out_ref):
        pre = jnp.zeros((count, lat_dev), F32)
        dec_sq = jnp.zeros((lat_dev, lat_dev), F32)
        for i in range(pieces):
            columns = slice(i * chunk, (i + 1) * chunk)
            rows = got_ref[:, :, columns].reshape(count, chunk).astype(F32)
            centered = (rows - bias_ref[:, columns]).astype(BF16)
            pre = pre + lax.dot_general(
                centered, enc_ref[:, columns], (((1,), (1,)), ((), ())), preferred_element_type=F32)
            dec_sq = dec_sq + folded(dec_ref[:, columns].astype(F32), lat_dev)
        fresh = jnp.zeros((owners, lat_dev), F32)
        for i in range(tok_dev):
            fresh = fresh + folded(got_ref[:, i, width:].astype(F32) - bias_ref[:, i * part : (i + 1) * part], lat_dev)
        fresh = jnp.sum(fresh, axis=1, keepdims=True)
        out_ref[:count, :] = pre
        out_ref[count : count + 1, :] = spread(jnp.sum(dec_sq, axis=1, keepdims=True), lat_dev)
        out_ref[count + 1 : count + 2, :] = squares_ref[0:1, :]
        for i in range(extra):
            out_ref[count + 2 + i : count + 3 + i, :] = spread(fresh[i * lanes : (i + 1) * lanes], lat_dev)
        out_ref[count + 2 + extra :, :] = squares_ref[1:, :]

    return pl.pallas_call(
        body,
        out_shape=pinned((count + 2 + extra + tok_dev, lat_dev), F32),
        in_specs=[pl.BlockSpec(memory_space=pltpu.VMEM)] * 5,
        out_specs=pl.BlockSpec(memory_space=pltpu.VMEM),
        name="compared",
    )(*in_vmem(got, b_dec, squares, w_enc, w_dec))


def encoded(own, peer, b_enc, mask, living, w_enc, w_dec, owners):
    count, lat_dev = mask.shape
    width = w_dec.shape[1]
    tok_dev = count // owners
    pieces = 4
    chunk = width // pieces

    def body(own_ref, peer_ref, bias_ref, mask_ref, living_ref, _, dec_ref, out_ref):
        total = own_ref[: count + 2, :] + peer_ref[: count + 2, :]
        codes = (jnp.maximum(total[:count] + bias_ref[...], 0.0) * mask_ref[...]).astype(BF16)
        for i in range(pieces):
            columns = slice(i * chunk, (i + 1) * chunk)
            part = jnp.dot(codes, dec_ref[:, columns], preferred_element_type=F32).astype(BF16)
            out_ref[:, :, columns] = part.reshape(owners, tok_dev, chunk)
        norms = jnp.sqrt(total[count : count + 2])
        alive = jnp.broadcast_to(norms[1:2] * living_ref[...], (count, lat_dev))
        side = jnp.concatenate([codes.astype(F32) * norms[0:1], alive], axis=1)
        high = side.astype(BF16)
        low = (side - high.astype(F32)).astype(BF16)
        out_ref[:, :, width:] = jnp.concatenate([high, low], axis=1).reshape(owners, tok_dev, 4 * lat_dev)

    shape = (owners, tok_dev, width + 4 * lat_dev)
    return pl.pallas_call(
        body,
        out_shape=(pltpu.VMEM if small(shape, BF16) else jax.ShapeDtypeStruct)(shape, BF16),
        in_specs=[pl.BlockSpec(memory_space=pltpu.VMEM)] * 7,
        out_specs=pl.BlockSpec(memory_space=pltpu.VMEM),
        name="encoded",
    )(*in_vmem(own, peer, b_enc, mask, living, w_enc, w_dec))


def finished(summed, got, b_dec, total, place, w_enc, w_dec, living, b_enc, moments, count):
    owners, tok_dev, _ = got.shape
    lat_dev, width = w_dec.shape
    part = width // tok_dev
    pieces = 2
    chunk = part // pieces
    steps = tok_dev * pieces

    def column(row, size):
        rows, lanes = (lax.broadcasted_iota(jnp.int32, (size, row.shape[1]), i) for i in range(2))
        return jnp.sum(jnp.where(rows == lanes, row, 0.0), axis=1, keepdims=True)

    def body(summed_ref, got_ref, bias_ref, total_ref, place_ref, enc_ref, dec_ref, living_ref, enc_bias_ref,
             moments_ref, new_enc_ref, new_dec_ref, new_bias_ref, new_moments_ref,
             enc_buffer, dec_buffer, bias_buffer, moments_buffer, sems):
        fetch = pltpu.make_async_copy(moments_ref, moments_buffer, sems.at[2 * steps])
        fetch.start()
        bias_buffer[...] = enc_bias_ref[...] * living_ref[...]
        first = width + lat_dev
        norms = summed_ref[0:1, first : first + lat_dev] + summed_ref[0:1, first + 2 * lat_dev : first + 3 * lat_dev]
        level = 0.2 * (jnp.sum(norms, axis=1, keepdims=True) / count)
        lanes = min(owners, lat_dev)
        fresh_sq = jnp.concatenate(
            [column(total_ref[2 + i : 3 + i, :], lanes) for i in range(owners // lanes)], axis=0)
        scale = lax.rsqrt(fresh_sq + EPS)
        again = lax.rsqrt(fresh_sq / (fresh_sq + EPS) + EPS)
        alive = lax.rsqrt(column(total_ref[0:1, :], lat_dev) + EPS)
        dead = jnp.sum(place_ref[...].astype(F32), axis=1, keepdims=True) > 0.0
        copies = []

        def send(buffer, out_ref, columns):
            copy = pltpu.make_async_copy(buffer.at[:, columns], out_ref.at[:, columns], sems.at[len(copies)])
            copy.start()
            copies.append(copy)

        for i in range(steps):
            columns = slice(i * chunk, (i + 1) * chunk)
            lane = width + i % pieces * chunk
            unit = (got_ref[:, i // pieces, lane : lane + chunk].astype(F32) - bias_ref[:, columns]) * scale
            placed = jnp.dot(place_ref[...], (level * unit).astype(BF16), preferred_element_type=F32)
            enc_buffer[:, columns] = jnp.where(dead, placed, enc_ref[:, columns].astype(F32)).astype(BF16)
            send(enc_buffer, new_enc_ref, columns)
            placed = jnp.dot(place_ref[...], (unit * again).astype(BF16), preferred_element_type=F32)
            dec_buffer[:, columns] = jnp.where(dead, placed, dec_ref[:, columns].astype(F32) * alive).astype(BF16)
            send(dec_buffer, new_dec_ref, columns)
        fetch.wait()
        moments_buffer[...] = moments_buffer[...] * living_ref[...]
        for i, (buffer, out_ref) in enumerate(((bias_buffer, new_bias_ref), (moments_buffer, new_moments_ref))):
            copy = pltpu.make_async_copy(buffer, out_ref, sems.at[2 * steps + 1 + i])
            copy.start()
            copies.append(copy)
        for copy in copies:
            copy.wait()

    like = jax.ShapeDtypeStruct(w_dec.shape, BF16)
    return pl.pallas_call(
        body,
        out_shape=(like, like, *(jax.ShapeDtypeStruct(x.shape, F32) for x in (b_enc, moments))),
        in_specs=[pl.BlockSpec(memory_space=pltpu.VMEM)] * 9 + [pl.BlockSpec(memory_space=pl.ANY)],
        out_specs=[pl.BlockSpec(memory_space=pl.ANY)] * 4,
        scratch_shapes=[pltpu.VMEM(w_dec.shape, BF16)] * 2 + [pltpu.VMEM(x.shape, F32) for x in (b_enc, moments)]
        + [pltpu.SemaphoreType.DMA((2 * steps + 3,))],
        name="finished",
    )(*in_vmem(summed, got, b_dec, total, place, w_enc, w_dec, living, b_enc), moments)


def lost(error, peer_error, total, summed, latents):
    tok_dev, lat_dev = error.shape
    width = summed.shape[1] - 4 * lat_dev
    full = width * lax.axis_size("hidden")

    def body(error_ref, peer_ref, total_ref, summed_ref, out_ref):
        mean_error = jnp.sum(error_ref[...] + peer_ref[...], axis=1, keepdims=True) / full
        mean_input = jnp.sum(total_ref[total_ref.shape[0] - tok_dev :, :], axis=1, keepdims=True) / full
        terms = summed_ref[:, width : width + lat_dev] + summed_ref[:, width + 2 * lat_dev : width + 3 * lat_dev]
        penalty = jnp.sum(terms, axis=1, keepdims=True)
        column = mean_error / (mean_input + EPS) + 5.0 * penalty / latents
        down, along = (lax.broadcasted_iota(jnp.int32, (tok_dev, tok_dev), i) for i in range(2))
        out_ref[...] = jnp.sum(jnp.where(down == along, column, 0.0), axis=0, keepdims=True)

    return pl.pallas_call(
        body,
        out_shape=jax.ShapeDtypeStruct((1, tok_dev), F32),
        in_specs=[pl.BlockSpec(memory_space=pltpu.VMEM)] * 4,
        out_specs=pl.BlockSpec(memory_space=pltpu.VMEM),
        name="lost",
    )(*in_vmem(error, peer_error, total, summed))[0]


def local(tokens, b_dec, w_enc, b_enc, w_dec, bias_moments, pool, active_blocks, dead_ids, row_ids):
    lat_dev, width = w_enc.shape
    owners = lax.axis_size("latent")
    tok_dev = tokens.shape[0]
    latents, count = lat_dev * owners, tok_dev * owners
    dead = dead_ids.shape[0]
    order = member_order(owners)
    members = jnp.array(order, jnp.int32)[:, None]

    sent, mask, place, living, centered, squares, b_dec, b_enc, w_enc, w_dec = prepared(
        tokens, pool, dead_ids[None], row_ids[None], members, active_blocks, b_enc[None], b_dec[None], w_enc, w_dec)
    got = lax.all_to_all(sent, "latent", 0, 0, axis_index_groups=[order])
    message = compared(got, b_dec, squares, w_enc, w_dec)
    peer = swap(message)
    sent = encoded(message, peer, b_enc, mask, living, w_enc, w_dec, owners)
    summed = lax.all_to_all(sent, "latent", 0, 0, axis_index_groups=[order])
    summed, got, message, peer = lax.optimization_barrier((summed, got, message, peer))
    total = message[count:] + peer[count:]
    summed = jnp.sum(summed.astype(F32), axis=0)
    residual = centered - summed[:, :width]
    error_part = jnp.sum(jnp.square(residual).reshape(tok_dev, -1, 128), axis=1)
    error_peer = swap(error_part)
    new_enc, new_dec, new_b_enc, new_moments = finished(
        summed, got, b_dec, total, place, w_enc, w_dec, living, b_enc, bias_moments, latents - dead)
    error_peer, new_enc, new_dec = lax.optimization_barrier((error_peer, new_enc, new_dec))
    losses = lost(error_part, error_peer, total, summed, latents)
    return losses, new_enc, new_dec, new_b_enc[0], new_moments


def solution(mesh):
    both = P(("groups", "latent"), "hidden")
    one = P(("groups", "latent"))
    return jax.shard_map(
        local,
        mesh=mesh,
        in_specs=(both, P(("groups", "hidden")), both, one, both, P(None, ("groups", "latent")), both,
                  P("groups", None), P("groups"), P("groups")),
        out_specs=(one, both, both, one, P(None, ("groups", "latent"))),
        check_vma=False,
    )
```
